256 devices in a mesh: rep: 16 (over z_hi, x), fsdp: 16 (over z_lo, y, core).
Axes of the slice: x: 4, y: 4, z: 8 (z_hi: 4, z_lo: 2; z = z_hi * 2 + z_lo), core: 2. Of those that a mesh axis runs over, the one named last changes fastest.
Arguments:
- layer_input: bfloat16 [16, 2, 4096, 5120], P('rep', None, 'fsdp'), may hold values from -6 to 6
- cotangent: bfloat16 [16, 2, 4096, 512], P('rep', None, 'fsdp'), may hold values from -6 to 6
- key_weight: bfloat16 [16, 5120, 512], P('rep', 'fsdp'), may hold values from -6 to 6
- key_gain: float32 [512], replicated, may hold values from 0.1 to 1.9
- fragment: bfloat16 [16, 5120, 512], P('rep', 'fsdp'), may hold values from -6 to 6
- outer_params: float32 [5120, 512], P('fsdp', 'rep'), may hold values from -6 to 6
- outer_momentum: float32 [5120, 512], P('fsdp', 'rep'), may hold values from -3 to 3
- plan: int32 [1], replicated, may hold values from 0 to 63
Outputs:
- new_key_weight: bfloat16 [16, 5120, 512], P('rep', 'fsdp')
- new_fragment: bfloat16 [16, 5120, 512], P('rep', 'fsdp')
- new_outer: float32 [5120, 512], P('fsdp', 'rep')
- new_momentum: float32 [5120, 512], P('fsdp', 'rep')
The draws below stay inside these ranges and needn't reach their ends.
All inputs are finite; a program needn't handle non-finite values.
Results may differ from the reference program's by a relative error of at most 0.014.
Values may be sent and summed in bfloat16 or wider, within the bound.
A program may use at most 128 MiB of HBM per device.

```python
import math
import jax
import jax.numpy as jnp
from jax import lax

D = 5120
HD = 128
TOK_DEV = 256
STEPS = 2
ROUNDS = 64
KC = 512
TOKENS = 4096
N_REP = 16
N_FSDP = 16


def raised(entries, own_key, source, target, shards_of, factor):
    def block_of(position):
        return (jnp.arange(entries.shape[position]) // (entries.shape[position] // shards_of)).reshape((-1,) + (1,) * (entries.ndim - 1 - position))

    first = jax.random.permutation(own_key, shards_of)[block_of(target)]
    other_side = (block_of(target) + shards_of // 2) % shards_of
    return jnp.where((block_of(source) == first) | (block_of(source) == other_side), factor * entries, entries)


def shard_levels(rng, dims, pieces, least, top_value):
    def one(position, shards_of):
        steps = jax.random.uniform(jax.random.fold_in(jax.random.fold_in(rng, 6), position), (shards_of,), jnp.float32, least / len(pieces), top_value / len(pieces))
        return jnp.repeat(jnp.exp(steps), dims[position] // shards_of).reshape((-1,) + (1,) * (len(dims) - position - 1))

    level = one(*pieces[0])
    for cut in pieces[1:]:
        level = level * one(*cut)
    return level


def centred(own_key, dims, width, most, cuts=(), held_as=jnp.bfloat16):
    array = width * jax.random.normal(own_key, dims, jnp.float32)
    if cuts:
        array = array * shard_levels(own_key, dims, cuts, -0.22, 0.18)
    return jnp.clip(array, -most, most).astype(held_as)


def bell_draw_with(stream_key, shape, deviation, most, cuts, heavy, held_as=jnp.bfloat16):
    result = deviation * jax.random.normal(stream_key, shape, jnp.float32)
    if cuts:
        result = result * shard_levels(stream_key, shape, cuts, -0.22, 0.18)
    return jnp.clip(raised(result, jax.random.fold_in(stream_key, 3), *heavy), -most, most).astype(held_as)


def setup_inputs(seed: int = 0) -> dict:
    arg_keys = jax.random.split(jax.random.key(seed), 9)
    layer_input = centred(arg_keys[0], (N_REP, STEPS, TOKENS, D), 1.0, 6.0, ((0, 16), (2, 16)))
    cotangent = centred(arg_keys[1], (N_REP, STEPS, TOKENS, KC), 1.0, 6.0, ((0, 16), (2, 16)))
    key_weight = centred(arg_keys[2], (N_REP, D, KC), 1.0, 6.0, ((0, 16), (1, 16)))
    key_gain = jnp.clip(1.0 + 0.18 * jax.random.normal(arg_keys[3], (KC,), jnp.float32), 0.1, 1.9)
    fragment = bell_draw_with(arg_keys[4], (N_REP, D, KC), 1.0, 6.0, ((0, 16), (1, 16)), (0, 2, 16, 2.0))
    outer_params = centred(arg_keys[5], (D, KC), 1.0, 6.0, ((0, 16), (1, 16)), jnp.float32)
    outer_momentum = centred(arg_keys[6], (D, KC), 0.5, 3.0, ((0, 16), (1, 16)), jnp.float32)
    plan = jax.random.randint(arg_keys[7], (1,), 0, ROUNDS).astype(jnp.int32)
    return dict(layer_input=layer_input, cotangent=cotangent, key_weight=key_weight, key_gain=key_gain, fragment=fragment, outer_params=outer_params, outer_momentum=outer_momentum, plan=plan)


MOMENTUM_DECAY = 0.9
OUTER_RATE = 0.7
LOCAL_SHARE = 0.25

def key_backward(key_values, cot_rows, key_gain):
    head_count = key_values.shape[1] // HD
    heads_view = key_values.reshape(key_values.shape[0], head_count, HD)
    root_mean = jnp.sqrt(lax.optimization_barrier(jnp.mean(heads_view * heads_view, axis=-1, keepdims=True)) + 1e-06)
    normalized = heads_view / root_mean
    pulled = cot_rows.astype(jnp.float32).reshape(heads_view.shape) * key_gain.reshape(head_count, HD)
    key_slope = (pulled - normalized * lax.optimization_barrier(jnp.mean(pulled * normalized, axis=-1, keepdims=True))) / root_mean
    return key_slope.reshape(key_values.shape).astype(jnp.bfloat16)

def shard_sum(inputs, key_slope, key_scale):
    blocks_in = inputs.reshape(N_FSDP, TOK_DEV, inputs.shape[1])
    blocks_slope = key_slope.reshape(N_FSDP, TOK_DEV, key_slope.shape[1])

    def accumulate(summed, pair):
        partial_value = key_scale * lax.dot_general(pair[0], pair[1], (((0,), (0,)), ((), ())), preferred_element_type=jnp.float32)
        rounded = lax.optimization_barrier(partial_value.astype(jnp.bfloat16))
        return (summed + rounded.astype(jnp.float32), None)
    summed, unused = lax.scan(accumulate, jnp.zeros((inputs.shape[1], key_slope.shape[1]), jnp.float32), (blocks_in, blocks_slope))
    return summed

def nesterov(outer_old, moment, group_mean, outer_factor):
    pseudo_grad = outer_old - group_mean
    moment_new = MOMENTUM_DECAY * moment + pseudo_grad
    outer_new = outer_old - outer_factor * (pseudo_grad + MOMENTUM_DECAY * moment_new)
    return (outer_new, moment_new)

def reference(layer_input, cotangent, key_weight, key_gain, fragment, outer_params, outer_momentum, plan):
    key_scale = D ** (-0.5)
    inner_rate = 0.5 * math.sqrt(D / TOKENS)

    def group_steps(operands):
        inputs, cot_steps, weight = operands
        for inner_step in range(STEPS):
            key_values = jnp.dot(inputs[inner_step], weight, preferred_element_type=jnp.float32) * key_scale
            key_slope = key_backward(key_values, cot_steps[inner_step], key_gain)
            gradient = shard_sum(inputs[inner_step], key_slope, key_scale)
            weight = (weight.astype(jnp.float32) - inner_rate * gradient).astype(jnp.bfloat16)
        return weight
    new_weight = lax.map(group_steps, (layer_input, cotangent, key_weight))
    frag_wide = fragment.astype(jnp.float32)
    group_mean = lax.optimization_barrier(jnp.sum(frag_wide, axis=0)) / N_REP
    outer_factor = OUTER_RATE * (0.55 + 0.45 * jnp.cos(math.pi * plan[0].astype(jnp.float32) / ROUNDS))
    new_outer, new_moment = nesterov(outer_params, outer_momentum, group_mean, outer_factor)
    blended = (LOCAL_SHARE * frag_wide + (1.0 - LOCAL_SHARE) * new_outer[None]).astype(jnp.bfloat16)
    return (new_weight, blended, new_outer, new_moment)
```

```python
import functools
import math

import jax
import jax.numpy as jnp
from jax import lax
from jax.experimental import pallas as pl
from jax.experimental.pallas import tpu as pltpu
from jax.sharding import PartitionSpec as P

D = 5120
HD = 128
STEPS = 2
ROUNDS = 64
MOMENTUM_DECAY = 0.9
OUTER_RATE = 0.7
LOCAL_SHARE = 0.25

MESH = pl.DeviceIdType.MESH
F32, BF16 = jnp.float32, jnp.bfloat16
NY, NZ = 4, 2
TOK = 256
ROWS = 320
SHARE = 2 * ROWS
CUT = 384
FR = 80


def add(*terms):
    total = terms[0].astype(F32)
    for term in terms[1:]:
        total = total + term.astype(F32)
    return total


def kernel(
    inner_rate,
    x_hbm,
    c_hbm,
    w_hbm,
    gain_ref,
    f_hbm,
    op_hbm,
    om_hbm,
    plan_ref,
    ow_hbm,
    of_hbm,
    oo_hbm,
    omn_hbm,
    xb,
    cb,
    wg,
    keys,
    slope_t,
    gp,
    gq,
    rp1,
    rp2,
    tpz,
    rp3,
    rq1,
    rq2,
    rq3,
    wout,
    fr,
    opb,
    omb,
    rf1,
    tf2,
    rf2,
    rf3,
    tf4,
    rf4,
    rf5,
    rf6,
    fout,
    oob,
    omnb,
    send_sems,
    recv_sems,
    local_sems,
):
    rep, fs = lax.axis_index("rep"), lax.axis_index("fsdp")
    z, y, c = fs // 8, (fs // 2) % 4, fs % 2
    zh, x = rep // 4, rep % 4
    yp, ym, y2 = (y + 1) % 4, (y + 3) % 4, (y + 2) % 4
    zo, co = 1 - z, 1 - c

    def dev(dz=z, dy=y, dc=c):
        return (rep, dz * 8 + dy * 2 + dc)

    up, down, across, twin = dev(dy=yp), dev(dy=ym), dev(dz=zo), dev(dc=co)
    xs = [(x + d) % 4 for d in (1, 2, 3)]
    zs = [(zh + d) % 4 for d in (1, 2, 3)]
    xdev = [(zh * 4 + i, fs) for i in xs]
    zdev = [(i * 4 + x, fs) for i in zs]

    started, locals_started = [], []

    def send(src, dst, to):
        i = len(started)
        copy = pltpu.make_async_remote_copy(
            src_ref=src,
            dst_ref=dst,
            send_sem=send_sems.at[i],
            recv_sem=recv_sems.at[i],
            device_id=to,
            device_id_type=MESH,
        )
        copy.start()
        started.append(copy)
        return copy

    def local(src, dst):
        copy = pltpu.make_async_copy(src, dst, local_sems.at[len(locals_started)])
        copy.start()
        locals_started.append(copy)
        return copy

    def columns(head):
        return pl.ds(pl.multiple_of(head * HD, HD), HD)

    half = lambda core: pl.ds(pl.multiple_of(core * 2 * HD, 2 * HD), 2 * HD)
    own_rows = pl.ds(pl.multiple_of(c * ROWS, 64), ROWS)
    other_rows = pl.ds(pl.multiple_of(co * ROWS, 64), ROWS)

    w_local = [local(w_hbm.at[0, :, columns(2 * c + h)], wg.at[0, h, z, y, own_rows, :]) for h in range(2)]
    x_local = [local(x_hbm.at[0, 0], xb.at[0, pl.ds(0, TOK), :]), None]
    c_local = [local(c_hbm.at[0, s, :, half(c)], cb.at[s, pl.ds(0, TOK), :]) for s in range(STEPS)]
    x_local[1] = local(x_hbm.at[0, 1], xb.at[1, pl.ds(0, TOK), :])
    f_local = local(f_hbm.at[0], fr)
    op_local = local(op_hbm, opb)
    om_local = local(om_hbm, omb)

    barrier = pltpu.get_barrier_semaphore()
    greeted = [twin, up, down, across] + xdev + zdev
    for to in greeted:
        pl.semaphore_signal(barrier, inc=1, device_id=to, device_id_type=MESH)
    pl.semaphore_wait(barrier, len(greeted))

    w_swap = [
        send(w_hbm.at[0, :, columns(2 * co + h)], wg.at[0, h, z, y, own_rows, :], twin) for h in range(2)
    ]
    x_swap, c_swap = [], []
    for s in range(STEPS):
        x_swap.append(send(x_hbm.at[0, s], xb.at[s, pl.ds(TOK, TOK), :], twin))
        c_swap.append(send(c_hbm.at[0, s, :, half(co)], cb.at[s, pl.ds(TOK, TOK), :], twin))

    class Gather:
        def __init__(self, s, h):
            self.w = wg.at[s, h]

        def block(self, bz, by, at, size):
            return self.w.at[bz, by, pl.ds(at, size), :]

        def push(self, bz, by, at, size, to):
            ref = self.block(bz, by, at, size)
            return send(ref, ref, to)

        def first(self):
            p, q = (0, CUT), (CUT, SHARE - CUT)
            self.pz = self.push(z, y, *p, across)
            self.qu = self.push(z, y, *q, up)
            self.qd = self.push(z, y, *q, down)
            self.pu = self.push(z, y, *p, up)
            self.pd = self.push(z, y, *p, down)
            self.qz = self.push(z, y, *q, across)

        def second(self):
            p, q = (0, CUT), (CUT, SHARE - CUT)
            hp, hq = CUT // 2, (SHARE - CUT) // 2
            self.qu.wait_recv()
            self.quz = self.push(z, ym, *q, across)
            self.quu = self.push(z, ym, CUT, hq, up)
            self.qd.wait_recv()
            self.qdz = self.push(z, yp, *q, across)
            self.qdd = self.push(z, yp, CUT + hq, hq, down)
            self.pz.wait_recv()
            self.pzu = self.push(zo, y, *p, up)
            self.pzd = self.push(zo, y, *p, down)
            self.pu.wait_recv()
            self.puu = self.push(z, ym, 0, hp, up)
            self.pd.wait_recv()
            self.pdd = self.push(z, yp, hp, hp, down)

        def third(self):
            hp, hq = CUT // 2, (SHARE - CUT) // 2
            self.quu.wait_recv()
            self.quuz = self.push(z, y2, CUT, hq, across)
            self.qdd.wait_recv()
            self.qddz = self.push(z, y2, CUT + hq, hq, across)
            self.pzu.wait_recv()
            self.pzuu = self.push(zo, ym, 0, hp, up)
            self.pzd.wait_recv()
            self.pzdd = self.push(zo, yp, hp, hp, down)

        def finish(self):
            for copy in (
                self.qz, self.quz, self.qdz, self.puu, self.pdd,
                self.quuz, self.qddz, self.pzuu, self.pzdd,
            ):
                copy.wait_recv()

    class Scatter:
        def __init__(self, s, h):
            self.s, self.h = s, h
            self.gp, self.gq = gp.at[s, h], gq.at[s, h]
            self.rp1, self.rp2, self.rp3 = rp1.at[s, h], rp2.at[s, h], rp3.at[s, h]
            self.tpz = tpz.at[s, h]
            self.rq1, self.rq2, self.rq3 = rq1.at[s, h], rq2.at[s, h], rq3.at[s, h]

        def grad(self, by):
            lhs = slope_t[self.h]

            def one(bz, carry):
                at = pl.multiple_of((bz * NY + by) * SHARE, HD)
                part = jnp.dot(lhs, xb[self.s, :, pl.ds(at, SHARE)], preferred_element_type=F32)
                self.gp[bz, by] = part[:, :CUT].astype(BF16)
                self.gq[bz, by] = part[:, CUT:].astype(BF16)
                return carry

            lax.fori_loop(0, NZ, one, 0)

        def first(self):
            lo, hi = pl.ds(0, HD // 2), pl.ds(HD // 2, HD // 2)
            self.grad(y2)
            self.z2 = send(self.gq.at[zo, y2], self.rq1.at[y2], across)
            self.pu = send(self.gp.at[:, y2, lo], self.rp1.at[0], up)
            self.pd = send(self.gp.at[:, y2, hi], self.rp1.at[1], down)
            self.grad(yp)
            self.zp = send(self.gq.at[zo, yp], self.rq1.at[yp], across)
            self.pu1 = send(self.gp.at[:, yp, hi], self.rp2.at[0, :, hi], up)
            self.grad(ym)
            self.zm = send(self.gq.at[zo, ym], self.rq1.at[ym], across)
            self.pd1 = send(self.gp.at[:, ym, lo], self.rp2.at[1, :, lo], down)
            self.grad(y)
            self.z0 = send(self.gq.at[zo, y], self.rq1.at[y], across)

        def second(self):
            lo, hi = pl.ds(0, HD // 2), pl.ds(HD // 2, HD // 2)
            self.z2.wait_recv()
            self.rq1[y2] = add(self.rq1[y2], self.gq[z, y2]).astype(BF16)
            self.qu = send(self.rq1.at[y2, lo], self.rq2.at[0], up)
            self.qd = send(self.rq1.at[y2, hi], self.rq2.at[1], down)
            self.pu.wait_recv()
            self.rp1[0] = add(self.rp1[0], self.gp[:, yp, lo]).astype(BF16)
            self.pu2 = send(self.rp1.at[0], self.rp2.at[0, :, lo], up)
            self.pd.wait_recv()
            self.rp1[1] = add(self.rp1[1], self.gp[:, ym, hi]).astype(BF16)
            self.pd2 = send(self.rp1.at[1], self.rp2.at[1, :, hi], down)
            self.zp.wait_recv()
            self.rq1[yp] = add(self.rq1[yp], self.gq[z, yp]).astype(BF16)
            self.qu1 = send(self.rq1.at[yp, hi], self.rq3.at[0, hi], up)
            self.zm.wait_recv()
            self.rq1[ym] = add(self.rq1[ym], self.gq[z, ym]).astype(BF16)
            self.qd1 = send(self.rq1.at[ym, lo], self.rq3.at[1, lo], down)

        def third(self):
            lo, hi = pl.ds(0, HD // 2), pl.ds(HD // 2, HD // 2)
            self.qu.wait_recv()
            self.rq1[yp, lo] = add(self.rq1[yp, lo], self.rq2[0]).astype(BF16)
            self.qu2 = send(self.rq1.at[yp, lo], self.rq3.at[0, lo], up)
            self.qd.wait_recv()
            self.rq1[ym, hi] = add(self.rq1[ym, hi], self.rq2[1]).astype(BF16)
            self.qd2 = send(self.rq1.at[ym, hi], self.rq3.at[1, hi], down)
            for copy in (self.pu1, self.pu2, self.pd1, self.pd2):
                copy.wait_recv()
            self.tpz[...] = add(self.gp[zo, y], self.rp2[0, zo], self.rp2[1, zo]).astype(BF16)
            self.zl = send(self.tpz, self.rp3, across)

        def finish(self):
            self.z0.wait_recv()
            for copy in (self.qu1, self.qu2, self.qd1, self.qd2):
                copy.wait_recv()
            q = add(self.gq[z, y], self.rq1[y], self.rq3[0], self.rq3[1])
            old = wg.at[self.s, self.h, z, y]
            new = wg.at[1, self.h, z, y] if self.s + 1 < STEPS else wout.at[self.h]
            scale = inner_rate * D**-0.5
            new[CUT:, :] = (old[CUT:, :].astype(F32) - scale * q.T).astype(BF16)
            self.zl.wait_recv()
            p = add(self.gp[z, y], self.rp2[0, z], self.rp2[1, z], self.rp3[...])
            new[:CUT, :] = (old[:CUT, :].astype(F32) - scale * p.T).astype(BF16)

    def project(s, h):
        def one(i, carry):
            at = pl.multiple_of(i * 2 * SHARE, HD)
            lhs = xb[s, :, pl.ds(at, 2 * SHARE)]
            bz, by = i // 2, 2 * (i % 2)
            rhs = wg[s, h, bz, pl.ds(by, 2)].reshape(2 * SHARE, HD)
            part = jnp.dot(lhs, rhs, preferred_element_type=F32)
            keys[...] = jnp.where(i == 0, part, keys[...] + part)
            return carry

        lax.fori_loop(0, NY * NZ // 2, one, 0)

    def backward(s, h):
        k = keys[...] * D**-0.5
        inverse = lax.rsqrt(jnp.mean(k * k, axis=-1, keepdims=True) + 1e-06)
        u = k * inverse
        gain = gain_ref[pl.ds(2 * c + h, 1), :]
        pulled = cb[s, :, h * HD : (h + 1) * HD].astype(F32) * gain
        slope = (pulled - u * jnp.mean(pulled * u, axis=-1, keepdims=True)) * inverse
        slope_t[h] = slope.T.astype(BF16)

    outer = {}

    def outer_0():
        outer["a"] = [send(f_hbm.at[0, pl.ds(pl.multiple_of(i * FR, 16), FR), :], rf1.at[n], to)
                      for n, (i, to) in enumerate(zip(xs, xdev))]

    def outer_1():
        f_local.wait()
        for copy in outer["a"]:
            copy.wait_recv()
        mine = fr[pl.ds(pl.multiple_of(x * FR, 16), FR), :]
        total = add(mine, rf1[0], rf1[1], rf1[2]).astype(BF16)
        for i in range(4):
            tf2[i] = total[:, i * HD : (i + 1) * HD]
        outer["b"] = [send(tf2.at[i], rf2.at[n], to) for n, (i, to) in enumerate(zip(zs, zdev))]

    def outer_2():
        for copy in outer["b"]:
            copy.wait_recv()
        rf3[x] = add(tf2[zh], rf2[0], rf2[1], rf2[2])
        outer["c"] = [send(rf3.at[x], rf3.at[x], to) for to in xdev]

    def outer_3():
        op_local.wait()
        om_local.wait()
        for copy in outer["c"]:
            copy.wait_recv()
        lane = lax.broadcasted_iota(jnp.int32, (FR, HD), 1)
        plan = jnp.full((8, HD), plan_ref[0].astype(F32))
        factor = (OUTER_RATE * (0.55 + 0.45 * jnp.cos(math.pi * plan / ROUNDS)))[:1]
        pick = lambda a: jnp.where(
            x < 2,
            jnp.where(x == 0, a[:, 0:32], a[:, 32:64]),
            jnp.where(x == 2, a[:, 64:96], a[:, 96:128]),
        )
        for i in range(4):
            rows = slice(i * FR, (i + 1) * FR)
            old = jnp.concatenate([opb[rows, :]] * 4, axis=1)
            moment = jnp.concatenate([omb[rows, :]] * 4, axis=1)
            pseudo = old - rf3[i] * (1.0 / 16)
            moment = MOMENTUM_DECAY * moment + pseudo
            new = old - factor * (pseudo + MOMENTUM_DECAY * moment)
            oob[rows, :] = pick(new)
            omnb[rows, :] = pick(moment)
            tf4[i] = jnp.where(lane // 32 == x, new, 0.0).astype(BF16)
        local(oob, oo_hbm)
        local(omnb, omn_hbm)
        outer["d"] = [send(tf4.at[i], rf4.at[n], to) for n, (i, to) in enumerate(zip(xs, xdev))]

    def outer_4():
        for copy in outer["d"]:
            copy.wait_recv()
        rf5[zh] = add(tf4[x], rf4[0], rf4[1], rf4[2]).astype(BF16)
        outer["e"] = [send(rf5.at[zh], rf5.at[zh], to) for to in zdev]

    def outer_5():
        for copy in outer["e"]:
            copy.wait_recv()
        outer["f"] = [send(rf5, rf6.at[x], to) for to in xdev]
        rf6[x] = rf5[...]

    def outer_6():
        for copy in outer["f"]:
            copy.wait_recv()
        for i in range(4):
            for j in range(4):
                rows, cols = slice(i * FR, (i + 1) * FR), slice(j * HD, (j + 1) * HD)
                blend = LOCAL_SHARE * fr[rows, cols].astype(F32)
                blend = blend + (1.0 - LOCAL_SHARE) * rf6[i, j].astype(F32)
                fout[rows, cols] = blend.astype(BF16)
        local(fout, of_hbm.at[0])

    def write(h):
        src = wout.at[h]
        local(src.at[own_rows, :], ow_hbm.at[0, :, columns(2 * c + h)])
        return send(src.at[other_rows, :], ow_hbm.at[0, :, columns(2 * c + h)], twin)

    ga, gb = [Gather(s, 0) for s in range(2)], [Gather(s, 1) for s in range(2)]
    sa, sb = [Scatter(s, 0) for s in range(2)], [Scatter(s, 1) for s in range(2)]

    w_local[0].wait()
    w_swap[0].wait_recv()
    ga[0].first()
    outer_0()
    w_local[1].wait()
    w_swap[1].wait_recv()
    ga[0].second()
    gb[0].first()
    ga[0].third()
    outer_1()
    gb[0].second()
    for s in range(STEPS):
        x_local[s].wait()
        x_swap[s].wait_recv()
        c_local[s].wait()
        c_swap[s].wait_recv()
        ga[s].finish()
        project(s, 0)
        backward(s, 0)
        gb[s].third()
        sa[s].first()
        outer_2() if s == 0 else outer_5()
        sa[s].second()
        gb[s].finish()
        project(s, 1)
        backward(s, 1)
        sa[s].third()
        sb[s].first()
        outer_3() if s == 0 else outer_6()
        sa[s].finish()
        if s == 0:
            ga[1].first()
            sb[0].second()
            ga[1].second()
            sb[0].third()
            ga[1].third()
            outer_4()
            sb[0].finish()
            gb[1].first()
            gb[1].second()
        else:
            out_a = write(0)
            sb[1].second()
            sb[1].third()
            sb[1].finish()
            out_b = write(1)
    out_a.wait_recv()
    out_b.wait_recv()
    for copy in locals_started[9:]:
        copy.wait()
    for copy in started:
        copy.wait_send()


def shards(
    layer_input, cotangent, key_weight, key_gain, fragment, outer_params, outer_momentum, plan
):
    tokens = layer_input.shape[2] * lax.axis_size("fsdp")
    inner_rate = 0.5 * math.sqrt(D / tokens)
    any_spec = pl.BlockSpec(memory_space=pl.ANY)
    vmem = lambda *shape, dtype=BF16: pltpu.VMEM(shape, dtype)
    hc, zr = HD // 2, SHARE - CUT
    return pl.pallas_call(
        functools.partial(kernel, inner_rate),
        out_shape=(
            jax.ShapeDtypeStruct(key_weight.shape, BF16),
            jax.ShapeDtypeStruct(fragment.shape, BF16),
            jax.ShapeDtypeStruct(outer_params.shape, F32),
            jax.ShapeDtypeStruct(outer_momentum.shape, F32),
        ),
        in_specs=[any_spec] * 3
        + [pl.BlockSpec(memory_space=pltpu.VMEM)]
        + [any_spec] * 3
        + [pl.BlockSpec(memory_space=pltpu.SMEM)],
        out_specs=[any_spec] * 4,
        scratch_shapes=[
            vmem(STEPS, 2 * TOK, D),
            vmem(STEPS, 2 * TOK, 2 * HD),
            vmem(STEPS, 2, NZ, NY, SHARE, HD),
            vmem(2 * TOK, HD, dtype=F32),
            vmem(2, HD, 2 * TOK),
            vmem(STEPS, 2, NZ, NY, HD, CUT),
            vmem(STEPS, 2, NZ, NY, HD, zr),
            vmem(STEPS, 2, 2, NZ, hc, CUT),
            vmem(STEPS, 2, 2, NZ, HD, CUT),
            vmem(STEPS, 2, HD, CUT),
            vmem(STEPS, 2, HD, CUT),
            vmem(STEPS, 2, NY, HD, zr),
            vmem(STEPS, 2, 2, hc, zr),
            vmem(STEPS, 2, 2, HD, zr),
            vmem(2, SHARE, HD),
            vmem(ROWS, 4 * HD),
            vmem(ROWS, 32, dtype=F32),
            vmem(ROWS, 32, dtype=F32),
            vmem(3, FR, 4 * HD),
            vmem(4, FR, HD),
            vmem(3, FR, HD),
            vmem(4, FR, HD, dtype=F32),
            vmem(4, FR, HD),
            vmem(3, FR, HD),
            vmem(4, FR, HD),
            vmem(4, 4, FR, HD),
            vmem(ROWS, 4 * HD),
            vmem(ROWS, 32, dtype=F32),
            vmem(ROWS, 32, dtype=F32),
            pltpu.SemaphoreType.DMA((180,)),
            pltpu.SemaphoreType.DMA((180,)),
            pltpu.SemaphoreType.DMA((16,)),
        ],
        compiler_params=pltpu.CompilerParams(
            collective_id=0, has_side_effects=True, vmem_limit_bytes=56 << 20
        ),
        cost_estimate=pl.CostEstimate(
            flops=4 * 2 * 256 * D * 512, bytes_accessed=8 << 20, transcendentals=0
        ),
    )(
        layer_input,
        cotangent,
        key_weight,
        key_gain.reshape(4, HD),
        fragment,
        outer_params,
        outer_momentum,
        plan,
    )


def solution(mesh):
    placed = (
        P("rep", None, "fsdp", None),
        P("rep", None, "fsdp", None),
        P("rep", "fsdp", None),
        P(),
        P("rep", "fsdp", None),
        P("fsdp", "rep"),
        P("fsdp", "rep"),
        P(),
    )
    return jax.shard_map(
        shards,
        mesh=mesh,
        in_specs=placed,
        out_specs=(
            P("rep", "fsdp", None),
            P("rep", "fsdp", None),
            P("fsdp", "rep"),
            P("fsdp", "rep"),
        ),
        check_vma=False,
    )
```

```python
import functools
import math

import jax
import jax.numpy as jnp
from jax import lax
from jax.experimental import pallas as pl
from jax.experimental.pallas import tpu as pltpu
from jax.sharding import PartitionSpec as P

D = 5120
HD = 128
STEPS = 2
ROUNDS = 64
MOMENTUM_DECAY = 0.9
OUTER_RATE = 0.7
LOCAL_SHARE = 0.25

ORDER = (
    51, 1, 2, 0, 50, 200, 52, 4, 3, 5, 55, 7, 54, 201, 9, 6, 53, 11, 57, 12,
    10, 8, 62, 61, 56, 63, 13, 14, 60, 59, 58, 15, 16, 17, 64, 18, 65, 66, 20, 22,
    68, 21, 69, 19, 67, 24, 202, 26, 23, 25, 74, 70, 27, 72, 71, 73, 28, 101, 102, 75,
    76, 29, 100, 203, 77, 104, 103, 78, 151, 105, 107, 106, 112, 79, 150, 108, 109, 111, 110, 152,
    204, 153, 154, 113, 114, 155, 157, 156, 162, 115, 116, 158, 159, 163, 160, 161, 118, 117, 164, 122,
    121, 165, 166, 120, 119, 167, 168, 205, 170, 172, 171, 127, 124, 169, 174, 123, 125, 126, 173, 177,
    176, 175, 206, 128, 129, 130, 178, 179, 180,
)

MESH = pl.DeviceIdType.MESH
F32, BF16 = jnp.float32, jnp.bfloat16
NY, NZ = 4, 2
TOK = 256
ROWS = 320
SHARE = 2 * ROWS
CUT = 384
TOP = 384
SENT, CAME = 15, 55
FR = 80


def add(*terms):
    total = terms[0].astype(F32)
    for term in terms[1:]:
        total = total + term.astype(F32)
    return total


def kernel(
    inner_rate,
    x_hbm,
    c_hbm,
    w_hbm,
    gain_hbm,
    f_hbm,
    op_hbm,
    om_hbm,
    plan_hbm,
    ow_hbm,
    of_hbm,
    oo_hbm,
    omn_hbm,
    xb,
    cb,
    wg,
    keys,
    slope_t,
    gp,
    gq,
    rp1,
    rp2,
    tpz,
    rp3,
    rq1,
    rq2,
    rq3,
    wout,
    fr,
    opb,
    omb,
    rf1,
    tf2,
    rf2,
    rf3,
    tf4,
    rf4,
    rf5,
    rf6,
    fout,
    oob,
    omnb,
    side,
    gain_ref,
    plan_ref,
    relay,
    send_sems,
    recv_sems,
    local_sems,
):
    rep, fs = lax.axis_index("rep"), lax.axis_index("fsdp")
    z, y, c = fs // 8, (fs // 2) % 4, fs % 2
    zh, x = rep // 4, rep % 4
    yp, ym, y2 = (y + 1) % 4, (y + 3) % 4, (y + 2) % 4
    zo, co = 1 - z, 1 - c

    def dev(dz=z, dy=y, dc=c):
        return (rep, dz * 8 + dy * 2 + dc)

    up, down, across, twin = dev(dy=yp), dev(dy=ym), dev(dz=zo), dev(dc=co)
    xs = [(x + d) % 4 for d in (1, 2, 3)]
    zs = [(zh + d) % 4 for d in (1, 2, 3)]
    xdev = [(zh * 4 + i, fs) for i in xs]
    zdev = [(i * 4 + x, fs) for i in zs]

    locals_started, came_at, sent_at = [], {}, {}

    def remote(src, dst, sent, came, to=twin):
        return pltpu.make_async_remote_copy(
            src_ref=src,
            dst_ref=dst,
            send_sem=send_sems.at[sent_at.setdefault(sent, len(sent_at))],
            recv_sem=recv_sems.at[came_at.setdefault(came, len(came_at))],
            device_id=to,
            device_id_type=MESH,
        )

    def send(src, dst, to, sent, came):
        remote(src, dst, sent, came, to).start()

    def landed(ref, came):
        remote(ref, ref, "x0", came).wait_recv()

    def left(ref, sent):
        remote(ref, ref, sent, "x0").wait_send()

    def local(src, dst):
        copy = pltpu.make_async_copy(src, dst, local_sems.at[len(locals_started)])
        copy.start()
        locals_started.append(copy)
        return copy

    def columns(head):
        return pl.ds(pl.multiple_of(head * HD, HD), HD)

    half = lambda core: pl.ds(pl.multiple_of(core * 2 * HD, 2 * HD), 2 * HD)
    own_rows = pl.ds(pl.multiple_of(c * ROWS, 64), ROWS)
    other_rows = pl.ds(pl.multiple_of(co * ROWS, 64), ROWS)

    barrier = pltpu.get_barrier_semaphore()
    plane = [(rep, z * 8 + yp * 2), (rep, z * 8 + ym * 2), (rep, zo * 8 + y * 2)]
    plane += [(zh * 4 + i, z * 8 + y * 2) for i in xs]
    depth = [(i * 4 + x, z * 8 + y * 2 + 1) for i in zs]
    for to in plane + depth:
        pl.semaphore_signal(barrier, inc=1, device_id=to, device_id_type=MESH)

    @pl.when(c == 1)
    def _():
        pl.semaphore_signal(barrier, inc=1, device_id=twin, device_id_type=MESH)

    w_local = [local(w_hbm.at[0, :, columns(2 * c + h)], wg.at[0, h, z, y, own_rows, :]) for h in range(2)]
    x_local = [local(x_hbm.at[0, 0], xb.at[0, pl.ds(0, TOK), :]), None]
    c_local = [local(c_hbm.at[0, s, :, half(c)], cb.at[s, pl.ds(0, TOK), :]) for s in range(STEPS)]
    x_local[1] = local(x_hbm.at[0, 1], xb.at[1, pl.ds(0, TOK), :])
    f_local = local(f_hbm.at[0], fr)
    op_local = local(op_hbm, opb)
    om_local = local(om_hbm, omb)
    gain_local = local(gain_hbm, gain_ref)
    plan_local = local(plan_hbm, plan_ref)

    @pl.when(c == 0)
    def _():
        pl.semaphore_wait(barrier, 2 * len(plane) + 1)
        pl.semaphore_signal(relay, inc=1, device_id=twin, device_id_type=MESH)

    @pl.when(c == 1)
    def _():
        pl.semaphore_wait(relay, 1)

    def meet_depth():
        @pl.when(c == 1)
        def _():
            pl.semaphore_wait(barrier, 2 * len(depth))
            pl.semaphore_signal(relay, inc=1, device_id=twin, device_id_type=MESH)

        @pl.when(c == 0)
        def _():
            pl.semaphore_wait(relay, 1)

    for h in range(2):
        dst = wg.at[0, h, z, y, own_rows, :]
        send(w_hbm.at[0, :, columns(2 * co + h)], dst, twin, "ws", "ws")
    send(x_hbm.at[0, 0], xb.at[0, pl.ds(TOK, TOK), :], twin, "x0", "x0")
    for s in range(STEPS):
        send(c_hbm.at[0, s, :, half(co)], cb.at[s, pl.ds(TOK, TOK), :], twin, "c", "c")
    send(x_hbm.at[0, 1], xb.at[1, pl.ds(TOK, TOK), :], twin, "x1", "x1")

    todo = {}
    lo, hi = pl.ds(0, HD // 2), pl.ds(HD // 2, HD // 2)
    groups = dict(puu="k3", pdd="k3", qdz="k3", quz="k4", quuz="k4", qddz="k4", pzuu="k4", pzdd="k4",
                  Pu1="rp", Pu2="rp", Pd1="rp", Pd2="rp", z0="uq", Qu1="uq", Qu2="uq", Qd1="uq", Qd2="uq")

    def inner(s, h):
        k, mine = "AB"[h], "AB"[h] + str(s)
        w, sl = wg.at[s, h], slope_t.at[h]
        mp, mq = gp.at[s, h], gq.at[s, h]
        p1, p2, p3, pz = rp1.at[s, h], rp2.at[s, h], rp3.at[s, h], tpz.at[s, h]
        q1, q2, q3 = rq1.at[s, h], rq2.at[s, h], rq3.at[s, h]
        acc = keys.at[h]
        first, rest = (0, TOP), (TOP, SHARE - TOP)
        hp, hq = TOP // 2, (SHARE - TOP) // 2

        def push(name, bz, by, at, size, to):
            ref = w.at[bz, by, pl.ds(at, size), :]
            send(ref, ref, to, mine, k + groups.get(name, name))

        def put(name, src, dst, to):
            send(src, dst, to, mine, k + groups.get(name, name))

        def take(name, ref):
            landed(ref, k + name)

        def rows(at, size):
            return w.at[z, y, pl.ds(at, size), :]

        def g_p():
            push("pz", z, y, *first, across)
            push("pu", z, y, *first, up)
            push("pd", z, y, *first, down)

        def g_q():
            push("qu", z, y, *rest, up)
            push("qd", z, y, *rest, down)

        def g_z():
            push("qz", z, y, *rest, across)

        def a_qu():
            take("qu", rows(*rest))
            push("quu", z, ym, TOP, hq, up)
            push("quz", z, ym, *rest, across)

        def a_qd():
            take("qd", rows(*rest))
            push("qdd", z, yp, TOP + hq, hq, down)
            push("qdz", z, yp, *rest, across)

        def a_pz():
            take("pz", rows(*first))
            push("pzu", zo, y, *first, up)
            push("pzd", zo, y, *first, down)

        def a_pu():
            take("pu", rows(*first))
            push("puu", z, ym, 0, hp, up)

        def a_pd():
            take("pd", rows(*first))
            push("pdd", z, yp, hp, hp, down)

        def a_quu():
            take("quu", rows(TOP, hq))
            push("quuz", z, y2, TOP, hq, across)

        def a_qdd():
            take("qdd", rows(TOP, hq))
            push("qddz", z, y2, TOP + hq, hq, across)

        def a_pzu():
            take("pzu", rows(*first))
            push("pzuu", zo, ym, 0, hp, up)

        def a_pzd():
            take("pzd", rows(*first))
            push("pzdd", zo, yp, hp, hp, down)

        def project(*blocks):
            at = [pl.ds(pl.multiple_of((bz * NY + by) * SHARE, HD), SHARE) for bz, by in blocks]
            lhs = jnp.concatenate([xb[s, :, cols] for cols in at], axis=1)
            rhs = jnp.concatenate([w[bz, by] for bz, by in blocks], axis=0)
            return jnp.dot(lhs, rhs, preferred_element_type=F32)

        def k1():
            if h == 0:
                x_local[s].wait()
                landed(xb.at[s, pl.ds(TOK, TOK), :], "x" + str(s))
            acc[...] = project((z, y), (z, yp))

        def k2():
            take("qz", rows(*rest))
            acc[...] += project((z, ym), (zo, y))

        def k3():
            take("k3", w.at[z, y])
            acc[...] += project((z, y2), (zo, yp))

        def k4():
            take("k4", cb.at[0, pl.ds(0, (2 * SHARE - TOP) // 2), :])
            if h == 0 and s == 0:
                c_local[0].wait()
                c_local[1].wait()
                landed(cb.at[0], "c")
                gain_local.wait()
            kv = (acc[...] + project((zo, ym), (zo, y2))) * D**-0.5
            inverse = lax.rsqrt(jnp.mean(kv * kv, axis=-1, keepdims=True) + 1e-06)
            u = kv * inverse
            gain = gain_ref[pl.ds(2 * c + h, 1), :]
            pulled = cb[s, :, h * HD : (h + 1) * HD].astype(F32) * gain
            slope = (pulled - u * jnp.mean(pulled * u, axis=-1, keepdims=True)) * inverse
            sl[...] = slope.T.astype(BF16)

        def grad(by):
            lhs = sl[...]

            def one(bz, carry):
                at = pl.multiple_of((bz * NY + by) * SHARE, HD)
                part = jnp.dot(lhs, xb[s, :, pl.ds(at, SHARE)], preferred_element_type=F32)
                mp[bz, by] = part[:, :CUT].astype(BF16)
                mq[bz, by] = part[:, CUT:].astype(BF16)
                return carry

            lax.fori_loop(0, NZ, one, 0)

        def g2():
            grad(y2)
            put("z2", mq.at[zo, y2], q1.at[y2], across)
            put("Pu", mp.at[:, y2, lo], p1.at[0], up)
            put("Pd", mp.at[:, y2, hi], p1.at[1], down)

        def gu():
            grad(yp)
            put("zp", mq.at[zo, yp], q1.at[yp], across)
            put("Pu1", mp.at[:, yp, hi], p2.at[0, :, hi], up)

        def gd():
            grad(ym)
            put("zm", mq.at[zo, ym], q1.at[ym], across)
            put("Pd1", mp.at[:, ym, lo], p2.at[1, :, lo], down)

        def g0():
            grad(y)
            put("z0", mq.at[zo, y], q1.at[y], across)

        def r_z2():
            take("z2", q1.at[y2])
            q1[y2] = add(q1[y2], mq[z, y2]).astype(BF16)
            put("Qu", q1.at[y2, lo], q2.at[0], up)
            put("Qd", q1.at[y2, hi], q2.at[1], down)

        def r_pu():
            take("Pu", p1.at[0])
            p1[0] = add(p1[0], mp[:, yp, lo]).astype(BF16)
            put("Pu2", p1.at[0], p2.at[0, :, lo], up)

        def r_pd():
            take("Pd", p1.at[1])
            p1[1] = add(p1[1], mp[:, ym, hi]).astype(BF16)
            put("Pd2", p1.at[1], p2.at[1, :, hi], down)

        def r_zp():
            take("zp", q1.at[yp])
            q1[yp] = add(q1[yp], mq[z, yp]).astype(BF16)
            put("Qu1", q1.at[yp, hi], q3.at[0, hi], up)

        def r_zm():
            take("zm", q1.at[ym])
            q1[ym] = add(q1[ym], mq[z, ym]).astype(BF16)
            put("Qd1", q1.at[ym, lo], q3.at[1, lo], down)

        def r_qu():
            take("Qu", q2.at[0])
            q1[yp, lo] = add(q1[yp, lo], q2[0]).astype(BF16)
            put("Qu2", q1.at[yp, lo], q3.at[0, lo], up)

        def r_qd():
            take("Qd", q2.at[1])
            q1[ym, hi] = add(q1[ym, hi], q2[1]).astype(BF16)
            put("Qd2", q1.at[ym, hi], q3.at[1, hi], down)

        def r_p():
            take("rp", p2)
            pz[...] = add(mp[zo, y], p2[0, zo], p2[1, zo]).astype(BF16)
            put("zl", pz, p3, across)

        old = w.at[z, y]
        new = wg.at[1, h, z, y] if s + 1 < STEPS else wout.at[h]
        scale = inner_rate * D**-0.5

        def uq():
            take("uq", q1.at[pl.ds(0, 3)])
            total = add(mq[z, y], q1[y], q3[0], q3[1])
            new[CUT:, :] = (old[CUT:, :].astype(F32) - scale * total.T).astype(BF16)

        def up_():
            take("zl", p3)
            total = add(mp[z, y], p2[0, z], p2[1, z], p3[...])
            new[:CUT, :] = (old[:CUT, :].astype(F32) - scale * total.T).astype(BF16)

        def write():
            src, cols = wout.at[h], columns(2 * c + h)
            local(src.at[own_rows, :], ow_hbm.at[0, :, cols])
            send(src.at[other_rows, :], ow_hbm.at[0, :, cols], twin, "w", "w")

        steps = dict(
            gp=g_p, gq=g_q, gz=g_z, a_qu=a_qu, a_qd=a_qd, a_pz=a_pz, a_pu=a_pu, a_pd=a_pd,
            a_quu=a_quu, a_qdd=a_qdd, a_pzu=a_pzu, a_pzd=a_pzd, k1=k1, k2=k2, k3=k3, k4=k4,
            g2=g2, gu=gu, gd=gd, g0=g0, r_z2=r_z2, r_pu=r_pu, r_pd=r_pd, r_zp=r_zp, r_zm=r_zm,
            r_qu=r_qu, r_qd=r_qd, r_p=r_p, uq=uq, up=up_, w=write,
        )
        for i, step in enumerate(steps.values()):
            todo[100 * s + 50 * h + i] = step

    for s in range(STEPS):
        for h in range(2):
            inner(s, h)

    def outer_0():
        for n, (i, to) in enumerate(zip(xs, xdev)):
            src = f_hbm.at[0, pl.ds(pl.multiple_of(i * FR, 16), FR), :]
            send(src, rf1.at[n], to, "a", "a")

    def outer_1():
        f_local.wait()
        landed(rf1, "a")
        mine = fr[pl.ds(pl.multiple_of(x * FR, 16), FR), :]
        total = add(mine, rf1[0], rf1[1], rf1[2]).astype(BF16)
        for i in range(4):
            tf2[i] = total[:, i * HD : (i + 1) * HD]
        meet_depth()
        for n, (i, to) in enumerate(zip(zs, zdev)):
            send(tf2.at[i], rf2.at[n], to, "b", "b")

    def outer_2():
        landed(rf2, "b")
        rf3[x] = add(tf2[zh], rf2[0], rf2[1], rf2[2])
        for to in xdev:
            send(rf3.at[x], rf3.at[x], to, "g", "g")

    def outer_3():
        op_local.wait()
        om_local.wait()
        plan_local.wait()
        landed(rf3.at[pl.ds(0, 3)], "g")
        plan = jnp.full((8, HD), plan_ref[0].astype(F32))
        factor = (OUTER_RATE * (0.55 + 0.45 * jnp.cos(math.pi * plan / ROUNDS)))[:1, :1]
        mine = pl.ds(pl.multiple_of(x * 32, 32), 32)
        side[...] = rf3[...].reshape(ROWS, HD).T
        pseudo = opb[...] - side[mine, :] * (1.0 / 16)
        moment = MOMENTUM_DECAY * omb[...] + pseudo
        new = opb[...] - factor * (pseudo + MOMENTUM_DECAY * moment)
        oob[...] = new
        omnb[...] = moment
        side[...] = jnp.zeros_like(side)
        side[mine, :] = new
        tf4[...] = side[...].T.astype(BF16).reshape(4, FR, HD)
        local(oob, oo_hbm)
        local(omnb, omn_hbm)
        for n, (i, to) in enumerate(zip(xs, xdev)):
            send(tf4.at[i], rf4.at[n], to, "d", "d")

    def outer_4():
        landed(rf4, "d")
        rf5[zh] = add(tf4[x], rf4[0], rf4[1], rf4[2]).astype(BF16)
        for to in zdev:
            send(rf5.at[zh], rf5.at[zh], to, "e", "e")

    def outer_5():
        landed(rf5.at[pl.ds(0, 3)], "e")
        for to in xdev:
            send(rf5, rf6.at[x], to, "f", "f")
        rf6[x] = rf5[...]

    def outer_6():
        landed(rf6.at[pl.ds(0, 3)], "f")
        for i in range(4):
            for j in range(4):
                rows, cols = slice(i * FR, (i + 1) * FR), slice(j * HD, (j + 1) * HD)
                blend = LOCAL_SHARE * fr[rows, cols].astype(F32)
                blend = blend + (1.0 - LOCAL_SHARE) * rf6[i, j].astype(F32)
                fout[rows, cols] = blend.astype(BF16)
        local(fout, of_hbm.at[0])

    for i, step in enumerate((outer_0, outer_1, outer_2, outer_3, outer_4, outer_5, outer_6)):
        todo[200 + i] = step
    for copy in w_local:
        copy.wait()
    landed(wg.at[0, 0, z, y], "ws")
    for number in ORDER:
        todo[number]()
    two_heads = ow_hbm.at[0, :, pl.ds(0, 2 * HD)]
    landed(two_heads, "w")
    for copy in locals_started[11:]:
        copy.wait()
    for sent in ("A0", "B0", "A1", "B1"):
        left(xb.at[0, pl.ds(0, 14 * SHARE * HD // D), :], sent)
    left(wg.at[0, 0, z, y], "ws")
    left(two_heads, "w")
    left(cb.at[0], "c")
    for s in range(STEPS):
        left(xb.at[s, pl.ds(TOK, TOK), :], "x" + str(s))
    for sent, ref in (("a", rf1), ("b", rf2), ("g", rf3.at[pl.ds(0, 3)]), ("d", rf4),
                      ("e", rf5.at[pl.ds(0, 3)]), ("f", rf6.at[pl.ds(0, 3)])):
        left(ref, sent)


def shards(
    layer_input, cotangent, key_weight, key_gain, fragment, outer_params, outer_momentum, plan
):
    tokens = layer_input.shape[2] * lax.axis_size("fsdp")
    inner_rate = 0.5 * math.sqrt(D / tokens)
    any_spec = pl.BlockSpec(memory_space=pl.ANY)
    vmem = lambda *shape, dtype=BF16: pltpu.VMEM(shape, dtype)
    hc, zr = HD // 2, SHARE - CUT
    results = pl.pallas_call(
        functools.partial(kernel, inner_rate),
        out_shape=(
            jax.ShapeDtypeStruct(key_weight.shape, BF16),
            jax.ShapeDtypeStruct(fragment.shape, BF16),
            jax.ShapeDtypeStruct(outer_params.shape[::-1], F32),
            jax.ShapeDtypeStruct(outer_momentum.shape[::-1], F32),
        ),
        in_specs=[any_spec] * 8,
        out_specs=[any_spec] * 4,
        scratch_shapes=[
            vmem(STEPS, 2 * TOK, D),
            vmem(STEPS, 2 * TOK, 2 * HD),
            vmem(STEPS, 2, NZ, NY, SHARE, HD),
            vmem(2, 2 * TOK, HD, dtype=F32),
            vmem(2, HD, 2 * TOK),
            vmem(STEPS, 2, NZ, NY, HD, CUT),
            vmem(STEPS, 2, NZ, NY, HD, zr),
            vmem(STEPS, 2, 2, NZ, hc, CUT),
            vmem(STEPS, 2, 2, NZ, HD, CUT),
            vmem(STEPS, 2, HD, CUT),
            vmem(STEPS, 2, HD, CUT),
            vmem(STEPS, 2, NY, HD, zr),
            vmem(STEPS, 2, 2, hc, zr),
            vmem(STEPS, 2, 2, HD, zr),
            vmem(2, SHARE, HD),
            vmem(ROWS, 4 * HD),
            vmem(32, ROWS, dtype=F32),
            vmem(32, ROWS, dtype=F32),
            vmem(3, FR, 4 * HD),
            vmem(4, FR, HD),
            vmem(3, FR, HD),
            vmem(4, FR, HD, dtype=F32),
            vmem(4, FR, HD),
            vmem(3, FR, HD),
            vmem(4, FR, HD),
            vmem(4, 4, FR, HD),
            vmem(ROWS, 4 * HD),
            vmem(32, ROWS, dtype=F32),
            vmem(32, ROWS, dtype=F32),
            vmem(HD, ROWS, dtype=F32),
            vmem(4, HD, dtype=F32),
            pltpu.SMEM((1,), jnp.int32),
            pltpu.SemaphoreType.REGULAR,
            pltpu.SemaphoreType.DMA((SENT,)),
            pltpu.SemaphoreType.DMA((CAME,)),
            pltpu.SemaphoreType.DMA((16,)),
        ],
        compiler_params=pltpu.CompilerParams(
            collective_id=0, has_side_effects=True, vmem_limit_bytes=56 << 20
        ),
        cost_estimate=pl.CostEstimate(
            flops=4 * 2 * 256 * D * 512, bytes_accessed=8 << 20, transcendentals=0
        ),
    )(
        layer_input,
        cotangent,
        key_weight,
        key_gain.reshape(4, HD),
        fragment,
        outer_params.T,
        outer_momentum.T,
        plan,
    )
    new_weight, new_fragment, new_outer, new_moment = pl.pallas_call(
        hand_over,
        out_shape=[jax.ShapeDtypeStruct(a.shape, a.dtype) for a in results],
        in_specs=[any_spec] * 4,
        out_specs=[any_spec] * 4,
        scratch_shapes=[pltpu.VMEM(a.shape, a.dtype) for a in results]
        + [pltpu.SemaphoreType.DMA((4,))] * 2,
    )(*results)
    return new_weight, new_fragment, new_outer.T, new_moment.T


def hand_over(*refs):
    n = (len(refs) - 2) // 3
    came, gone = refs[-2:]
    loads = [pltpu.make_async_copy(refs[i], refs[2 * n + i], came.at[i]) for i in range(n)]
    stores = [pltpu.make_async_copy(refs[2 * n + i], refs[n + i], gone.at[i]) for i in range(n)]
    for copy in loads:
        copy.start()
    for load, store in zip(loads, stores):
        load.wait()
        store.start()
    for copy in stores:
        copy.wait()


def solution(mesh):
    placed = (
        P("rep", None, "fsdp", None),
        P("rep", None, "fsdp", None),
        P("rep", "fsdp", None),
        P(),
        P("rep", "fsdp", None),
        P("fsdp", "rep"),
        P("fsdp", "rep"),
        P(),
    )
    return jax.shard_map(
        shards,
        mesh=mesh,
        in_specs=placed,
        out_specs=(
            P("rep", "fsdp", None),
            P("rep", "fsdp", None),
            P("fsdp", "rep"),
            P("fsdp", "rep"),
        ),
        check_vma=False,
    )
```

```python
import functools
import math

import jax
import jax.numpy as jnp
from jax import lax
from jax.experimental import pallas as pl
from jax.experimental.pallas import tpu as pltpu
from jax.sharding import PartitionSpec as P

D = 5120
HD = 128
STEPS = 2
ROUNDS = 64
MOMENTUM_DECAY = 0.9
OUTER_RATE = 0.7
LOCAL_SHARE = 0.25

ORDER = (
    1, 200, 0, 50, 3, 4, 5, 6, 7, 2, 51, 52, 9, 12, 201, 8, 10, 11, 55, 13,
    56, 57, 14, 53, 54, 62, 15, 16, 60, 17, 61, 58, 59, 63, 18, 64, 20, 22, 21, 19,
    65, 66, 68, 23, 25, 27, 67, 24, 202, 26, 71, 70, 72, 29, 100, 28, 74, 101, 69, 76,
    73, 77, 75, 102, 105, 203, 103, 107, 104, 106, 78, 151, 112, 79, 150, 111, 108, 113, 109, 152,
    110, 114, 154, 204, 153, 155, 156, 157, 162, 115, 116, 163, 158, 160, 161, 159, 117, 118, 164, 121,
    122, 165, 166, 168, 167, 119, 205, 170, 171, 172, 127, 120, 174, 169, 176, 124, 123, 173, 175, 177,
    125, 126, 129, 206, 178, 128, 130, 179, 180,
)

MESH = pl.DeviceIdType.MESH
F32, BF16 = jnp.float32, jnp.bfloat16
NY, NZ = 4, 2
TOK = 256
ROWS = 320
SHARE = 2 * ROWS
CUT = 384
TOP = 384
SENT, CAME = 15, 55
FR = 80


def add(*terms):
    total = terms[0].astype(F32)
    for term in terms[1:]:
        total = total + term.astype(F32)
    return total


def kernel(
    inner_rate,
    x_hbm,
    c_hbm,
    w_hbm,
    gain_hbm,
    f_hbm,
    op_hbm,
    om_hbm,
    plan_hbm,
    ow_hbm,
    of_hbm,
    oo_hbm,
    omn_hbm,
    xb,
    cb,
    wg,
    keys,
    slope_t,
    gp,
    gq,
    rp1,
    rp2,
    tpz,
    rp3,
    rq1,
    rq2,
    rq3,
    wout,
    fr,
    opb,
    omb,
    rf1,
    tf2,
    rf2,
    rf3,
    tf4,
    rf4,
    rf5,
    rf6,
    fout,
    oob,
    omnb,
    side,
    gain_ref,
    plan_ref,
    relay,
    send_sems,
    recv_sems,
    local_sems,
):
    rep, fs = lax.axis_index("rep"), lax.axis_index("fsdp")
    z, y, c = fs // 8, (fs // 2) % 4, fs % 2
    zh, x = rep // 4, rep % 4
    yp, ym, y2 = (y + 1) % 4, (y + 3) % 4, (y + 2) % 4
    zo, co = 1 - z, 1 - c

    def dev(dz=z, dy=y, dc=c):
        return (rep, dz * 8 + dy * 2 + dc)

    up, down, across, twin = dev(dy=yp), dev(dy=ym), dev(dz=zo), dev(dc=co)
    xs = [(x + d) % 4 for d in (1, 2, 3)]
    zs = [(zh + d) % 4 for d in (1, 2, 3)]
    xdev = [(zh * 4 + i, fs) for i in xs]
    zdev = [(i * 4 + x, fs) for i in zs]

    locals_started, came_at, sent_at = [], {}, {}

    def remote(src, dst, sent, came, to=twin):
        return pltpu.make_async_remote_copy(
            src_ref=src,
            dst_ref=dst,
            send_sem=send_sems.at[sent_at.setdefault(sent, len(sent_at))],
            recv_sem=recv_sems.at[came_at.setdefault(came, len(came_at))],
            device_id=to,
            device_id_type=MESH,
        )

    def send(src, dst, to, sent, came):
        remote(src, dst, sent, came, to).start()

    def landed(ref, came):
        remote(ref, ref, "x0", came).wait_recv()

    def left(ref, sent):
        remote(ref, ref, sent, "x0").wait_send()

    def local(src, dst):
        copy = pltpu.make_async_copy(src, dst, local_sems.at[len(locals_started)])
        copy.start()
        locals_started.append(copy)
        return copy

    def columns(head):
        return pl.ds(pl.multiple_of(head * HD, HD), HD)

    half = lambda core: pl.ds(pl.multiple_of(core * 2 * HD, 2 * HD), 2 * HD)
    own_rows = pl.ds(pl.multiple_of(c * ROWS, 64), ROWS)
    other_rows = pl.ds(pl.multiple_of(co * ROWS, 64), ROWS)

    barrier = pltpu.get_barrier_semaphore()
    plane = [(rep, z * 8 + yp * 2), (rep, z * 8 + ym * 2), (rep, zo * 8 + y * 2)]
    plane += [(zh * 4 + i, z * 8 + y * 2) for i in xs]
    depth = [(i * 4 + x, z * 8 + y * 2 + 1) for i in zs]
    for to in plane + depth:
        pl.semaphore_signal(barrier, inc=1, device_id=to, device_id_type=MESH)

    @pl.when(c == 1)
    def _():
        pl.semaphore_signal(barrier, inc=1, device_id=twin, device_id_type=MESH)

    w_local = [local(w_hbm.at[0, :, columns(2 * c + h)], wg.at[0, h, z, y, own_rows, :]) for h in range(2)]
    x_local = [local(x_hbm.at[0, 0], xb.at[0, pl.ds(0, TOK), :]), None]
    c_local = [local(c_hbm.at[0, s, :, half(c)], cb.at[s, pl.ds(0, TOK), :]) for s in range(STEPS)]
    x_local[1] = local(x_hbm.at[0, 1], xb.at[1, pl.ds(0, TOK), :])
    f_local = local(f_hbm.at[0], fr)
    op_local = local(op_hbm, opb)
    om_local = local(om_hbm, omb)
    gain_local = local(gain_hbm, gain_ref)
    plan_local = local(plan_hbm, plan_ref)

    @pl.when(c == 0)
    def _():
        pl.semaphore_wait(barrier, 2 * len(plane) + 1)
        pl.semaphore_signal(relay, inc=1, device_id=twin, device_id_type=MESH)

    @pl.when(c == 1)
    def _():
        pl.semaphore_wait(relay, 1)

    def meet_depth():
        @pl.when(c == 1)
        def _():
            pl.semaphore_wait(barrier, 2 * len(depth))
            pl.semaphore_signal(relay, inc=1, device_id=twin, device_id_type=MESH)

        @pl.when(c == 0)
        def _():
            pl.semaphore_wait(relay, 1)

    for h in range(2):
        dst = wg.at[0, h, z, y, own_rows, :]
        send(w_hbm.at[0, :, columns(2 * co + h)], dst, twin, "ws", "ws")
    send(x_hbm.at[0, 0], xb.at[0, pl.ds(TOK, TOK), :], twin, "x0", "x0")
    for s in range(STEPS):
        send(c_hbm.at[0, s, :, half(co)], cb.at[s, pl.ds(TOK, TOK), :], twin, "c", "c")
    send(x_hbm.at[0, 1], xb.at[1, pl.ds(TOK, TOK), :], twin, "x1", "x1")

    todo = {}
    lo, hi = pl.ds(0, HD // 2), pl.ds(HD // 2, HD // 2)
    groups = dict(puu="k3", pdd="k3", qdz="k3", quz="k4", quuz="k4", qddz="k4", pzuu="k4", pzdd="k4",
                  Pu1="rp", Pu2="rp", Pd1="rp", Pd2="rp", z0="uq", Qu1="uq", Qu2="uq", Qd1="uq", Qd2="uq")

    def inner(s, h):
        k, mine = "AB"[h], "AB"[h] + str(s)
        w, sl = wg.at[s, h], slope_t.at[h]
        mp, mq = gp.at[s, h], gq.at[s, h]
        p1, p2, p3, pz = rp1.at[s, h], rp2.at[s, h], rp3.at[s, h], tpz.at[s, h]
        q1, q2, q3 = rq1.at[s, h], rq2.at[s, h], rq3.at[s, h]
        acc = keys.at[h]
        first, rest = (0, TOP), (TOP, SHARE - TOP)
        hp, hq = TOP // 2, (SHARE - TOP) // 2

        def push(name, bz, by, at, size, to):
            ref = w.at[bz, by, pl.ds(at, size), :]
            send(ref, ref, to, mine, k + groups.get(name, name))

        def put(name, src, dst, to):
            send(src, dst, to, mine, k + groups.get(name, name))

        def take(name, ref):
            landed(ref, k + name)

        def rows(at, size):
            return w.at[z, y, pl.ds(at, size), :]

        def g_p():
            push("pz", z, y, *first, across)
            push("pu", z, y, *first, up)
            push("pd", z, y, *first, down)

        def g_q():
            push("qu", z, y, *rest, up)
            push("qd", z, y, *rest, down)

        def g_z():
            push("qz", z, y, *rest, across)

        def a_qu():
            take("qu", rows(*rest))
            push("quu", z, ym, TOP, hq, up)
            push("quz", z, ym, *rest, across)

        def a_qd():
            take("qd", rows(*rest))
            push("qdd", z, yp, TOP + hq, hq, down)
            push("qdz", z, yp, *rest, across)

        def a_pz():
            take("pz", rows(*first))
            push("pzu", zo, y, *first, up)
            push("pzd", zo, y, *first, down)

        def a_pu():
            take("pu", rows(*first))
            push("puu", z, ym, 0, hp, up)

        def a_pd():
            take("pd", rows(*first))
            push("pdd", z, yp, hp, hp, down)

        def a_quu():
            take("quu", rows(TOP, hq))
            push("quuz", z, y2, TOP, hq, across)

        def a_qdd():
            take("qdd", rows(TOP, hq))
            push("qddz", z, y2, TOP + hq, hq, across)

        def a_pzu():
            take("pzu", rows(*first))
            push("pzuu", zo, ym, 0, hp, up)

        def a_pzd():
            take("pzd", rows(*first))
            push("pzdd", zo, yp, hp, hp, down)

        def project(*blocks):
            at = [pl.ds(pl.multiple_of((bz * NY + by) * SHARE, HD), SHARE) for bz, by in blocks]
            lhs = jnp.concatenate([xb[s, :, cols] for cols in at], axis=1)
            rhs = jnp.concatenate([w[bz, by] for bz, by in blocks], axis=0)
            return jnp.dot(lhs, rhs, preferred_element_type=F32)

        def k1():
            if h == 0:
                x_local[s].wait()
                landed(xb.at[s, pl.ds(TOK, TOK), :], "x" + str(s))
            acc[...] = project((z, y), (z, yp))

        def k2():
            take("qz", rows(*rest))
            acc[...] += project((z, ym), (zo, y))

        def k3():
            take("k3", w.at[z, y])
            acc[...] += project((z, y2), (zo, yp))

        def k4():
            take("k4", cb.at[0, pl.ds(0, (2 * SHARE - TOP) // 2), :])
            if h == 0 and s == 0:
                c_local[0].wait()
                c_local[1].wait()
                landed(cb.at[0], "c")
                gain_local.wait()
            kv = (acc[...] + project((zo, ym), (zo, y2))) * D**-0.5
            inverse = lax.rsqrt(jnp.mean(kv * kv, axis=-1, keepdims=True) + 1e-06)
            u = kv * inverse
            gain = gain_ref[pl.ds(2 * c + h, 1), :]
            pulled = cb[s, :, h * HD : (h + 1) * HD].astype(F32) * gain
            slope = (pulled - u * jnp.mean(pulled * u, axis=-1, keepdims=True)) * inverse
            sl[...] = slope.T.astype(BF16)

        def grad(by):
            lhs = sl[...]

            def one(bz, carry):
                at = pl.multiple_of((bz * NY + by) * SHARE, HD)
                part = jnp.dot(lhs, xb[s, :, pl.ds(at, SHARE)], preferred_element_type=F32)
                mp[bz, by] = part[:, :CUT].astype(BF16)
                mq[bz, by] = part[:, CUT:].astype(BF16)
                return carry

            lax.fori_loop(0, NZ, one, 0)

        def g2():
            grad(y2)
            put("z2", mq.at[zo, y2], q1.at[y2], across)
            put("Pu", mp.at[:, y2, lo], p1.at[0], up)
            put("Pd", mp.at[:, y2, hi], p1.at[1], down)

        def gu():
            grad(yp)
            put("zp", mq.at[zo, yp], q1.at[yp], across)
            put("Pu1", mp.at[:, yp, hi], p2.at[0, :, hi], up)

        def gd():
            grad(ym)
            put("zm", mq.at[zo, ym], q1.at[ym], across)
            put("Pd1", mp.at[:, ym, lo], p2.at[1, :, lo], down)

        def g0():
            grad(y)
            put("z0", mq.at[zo, y], q1.at[y], across)

        def r_z2():
            take("z2", q1.at[y2])
            q1[y2] = add(q1[y2], mq[z, y2]).astype(BF16)
            put("Qu", q1.at[y2, lo], q2.at[0], up)
            put("Qd", q1.at[y2, hi], q2.at[1], down)

        def r_pu():
            take("Pu", p1.at[0])
            p1[0] = add(p1[0], mp[:, yp, lo]).astype(BF16)
            put("Pu2", p1.at[0], p2.at[0, :, lo], up)

        def r_pd():
            take("Pd", p1.at[1])
            p1[1] = add(p1[1], mp[:, ym, hi]).astype(BF16)
            put("Pd2", p1.at[1], p2.at[1, :, hi], down)

        def r_zp():
            take("zp", q1.at[yp])
            q1[yp] = add(q1[yp], mq[z, yp]).astype(BF16)
            put("Qu1", q1.at[yp, hi], q3.at[0, hi], up)

        def r_zm():
            take("zm", q1.at[ym])
            q1[ym] = add(q1[ym], mq[z, ym]).astype(BF16)
            put("Qd1", q1.at[ym, lo], q3.at[1, lo], down)

        def r_qu():
            take("Qu", q2.at[0])
            q1[yp, lo] = add(q1[yp, lo], q2[0]).astype(BF16)
            put("Qu2", q1.at[yp, lo], q3.at[0, lo], up)

        def r_qd():
            take("Qd", q2.at[1])
            q1[ym, hi] = add(q1[ym, hi], q2[1]).astype(BF16)
            put("Qd2", q1.at[ym, hi], q3.at[1, hi], down)

        def r_p():
            take("rp", p2)
            pz[...] = add(mp[zo, y], p2[0, zo], p2[1, zo]).astype(BF16)
            put("zl", pz, p3, across)

        old = w.at[z, y]
        new = wg.at[1, h, z, y] if s + 1 < STEPS else wout.at[h]
        scale = inner_rate * D**-0.5

        def uq():
            take("uq", q1.at[pl.ds(0, 3)])
            total = add(mq[z, y], q1[y], q3[0], q3[1])
            new[CUT:, :] = (old[CUT:, :].astype(F32) - scale * total.T).astype(BF16)

        def up_():
            take("zl", p3)
            total = add(mp[z, y], p2[0, z], p2[1, z], p3[...])
            new[:CUT, :] = (old[:CUT, :].astype(F32) - scale * total.T).astype(BF16)

        def write():
            src, cols = wout.at[h], columns(2 * c + h)
            local(src.at[own_rows, :], ow_hbm.at[0, :, cols])
            send(src.at[other_rows, :], ow_hbm.at[0, :, cols], twin, "w", "w")

        steps = dict(
            gp=g_p, gq=g_q, gz=g_z, a_qu=a_qu, a_qd=a_qd, a_pz=a_pz, a_pu=a_pu, a_pd=a_pd,
            a_quu=a_quu, a_qdd=a_qdd, a_pzu=a_pzu, a_pzd=a_pzd, k1=k1, k2=k2, k3=k3, k4=k4,
            g2=g2, gu=gu, gd=gd, g0=g0, r_z2=r_z2, r_pu=r_pu, r_pd=r_pd, r_zp=r_zp, r_zm=r_zm,
            r_qu=r_qu, r_qd=r_qd, r_p=r_p, uq=uq, up=up_, w=write,
        )
        for i, step in enumerate(steps.values()):
            todo[100 * s + 50 * h + i] = step

    for s in range(STEPS):
        for h in range(2):
            inner(s, h)

    def outer_0():
        for n, (i, to) in enumerate(zip(xs, xdev)):
            src = f_hbm.at[0, pl.ds(pl.multiple_of(i * FR, 16), FR), :]
            send(src, rf1.at[n], to, "a", "a")

    def outer_1():
        f_local.wait()
        landed(rf1, "a")
        mine = fr[pl.ds(pl.multiple_of(x * FR, 16), FR), :]
        total = add(mine, rf1[0], rf1[1], rf1[2]).astype(BF16)
        for i in range(4):
            tf2[i] = total[:, i * HD : (i + 1) * HD]
        meet_depth()
        for n, (i, to) in enumerate(zip(zs, zdev)):
            send(tf2.at[i], rf2.at[n], to, "b", "b")

    def outer_2():
        landed(rf2, "b")
        rf3[x] = add(tf2[zh], rf2[0], rf2[1], rf2[2])
        for to in xdev:
            send(rf3.at[x], rf3.at[x], to, "g", "g")

    def outer_3():
        op_local.wait()
        om_local.wait()
        plan_local.wait()
        landed(rf3.at[pl.ds(0, 3)], "g")
        plan = jnp.full((8, HD), plan_ref[0].astype(F32))
        factor = (OUTER_RATE * (0.55 + 0.45 * jnp.cos(math.pi * plan / ROUNDS)))[:1, :1]
        mine = pl.ds(pl.multiple_of(x * 32, 32), 32)
        side[...] = rf3[...].reshape(ROWS, HD).T
        pseudo = opb[...] - side[mine, :] * (1.0 / 16)
        moment = MOMENTUM_DECAY * omb[...] + pseudo
        new = opb[...] - factor * (pseudo + MOMENTUM_DECAY * moment)
        oob[...] = new
        omnb[...] = moment
        side[...] = jnp.zeros_like(side)
        side[mine, :] = new
        tf4[...] = side[...].T.astype(BF16).reshape(4, FR, HD)
        local(oob, oo_hbm)
        local(omnb, omn_hbm)
        for n, (i, to) in enumerate(zip(xs, xdev)):
            send(tf4.at[i], rf4.at[n], to, "d", "d")

    def outer_4():
        landed(rf4, "d")
        rf5[zh] = add(tf4[x], rf4[0], rf4[1], rf4[2]).astype(BF16)
        for to in zdev:
            send(rf5.at[zh], rf5.at[zh], to, "e", "e")

    def outer_5():
        landed(rf5.at[pl.ds(0, 3)], "e")
        for to in xdev:
            send(rf5, rf6.at[x], to, "f", "f")
        rf6[x] = rf5[...]

    def outer_6():
        landed(rf6.at[pl.ds(0, 3)], "f")
        for i in range(4):
            for j in range(4):
                rows, cols = slice(i * FR, (i + 1) * FR), slice(j * HD, (j + 1) * HD)
                blend = LOCAL_SHARE * fr[rows, cols].astype(F32)
                blend = blend + (1.0 - LOCAL_SHARE) * rf6[i, j].astype(F32)
                fout[rows, cols] = blend.astype(BF16)
        local(fout, of_hbm.at[0])

    for i, step in enumerate((outer_0, outer_1, outer_2, outer_3, outer_4, outer_5, outer_6)):
        todo[200 + i] = step
    for copy in w_local:
        copy.wait()
    landed(wg.at[0, 0, z, y], "ws")
    for number in ORDER:
        todo[number]()
    two_heads = ow_hbm.at[0, :, pl.ds(0, 2 * HD)]
    landed(two_heads, "w")
    for copy in locals_started[11:]:
        copy.wait()
    for sent in ("A0", "B0", "A1", "B1"):
        left(xb.at[0, pl.ds(0, 14 * SHARE * HD // D), :], sent)
    left(wg.at[0, 0, z, y], "ws")
    left(two_heads, "w")
    left(cb.at[0], "c")
    for s in range(STEPS):
        left(xb.at[s, pl.ds(TOK, TOK), :], "x" + str(s))
    for sent, ref in (("a", rf1), ("b", rf2), ("g", rf3.at[pl.ds(0, 3)]), ("d", rf4),
                      ("e", rf5.at[pl.ds(0, 3)]), ("f", rf6.at[pl.ds(0, 3)])):
        left(ref, sent)


def shards(
    layer_input, cotangent, key_weight, key_gain, fragment, outer_params, outer_momentum, plan
):
    tokens = layer_input.shape[2] * lax.axis_size("fsdp")
    inner_rate = 0.5 * math.sqrt(D / tokens)
    any_spec = pl.BlockSpec(memory_space=pl.ANY)
    vmem = lambda *shape, dtype=BF16: pltpu.VMEM(shape, dtype)
    hc, zr = HD // 2, SHARE - CUT
    results = pl.pallas_call(
        functools.partial(kernel, inner_rate),
        out_shape=(
            jax.ShapeDtypeStruct(key_weight.shape, BF16),
            jax.ShapeDtypeStruct(fragment.shape, BF16),
            jax.ShapeDtypeStruct(outer_params.shape[::-1], F32),
            jax.ShapeDtypeStruct(outer_momentum.shape[::-1], F32),
        ),
        in_specs=[any_spec] * 8,
        out_specs=[any_spec] * 4,
        scratch_shapes=[
            vmem(STEPS, 2 * TOK, D),
            vmem(STEPS, 2 * TOK, 2 * HD),
            vmem(STEPS, 2, NZ, NY, SHARE, HD),
            vmem(2, 2 * TOK, HD, dtype=F32),
            vmem(2, HD, 2 * TOK),
            vmem(STEPS, 2, NZ, NY, HD, CUT),
            vmem(STEPS, 2, NZ, NY, HD, zr),
            vmem(STEPS, 2, 2, NZ, hc, CUT),
            vmem(STEPS, 2, 2, NZ, HD, CUT),
            vmem(STEPS, 2, HD, CUT),
            vmem(STEPS, 2, HD, CUT),
            vmem(STEPS, 2, NY, HD, zr),
            vmem(STEPS, 2, 2, hc, zr),
            vmem(STEPS, 2, 2, HD, zr),
            vmem(2, SHARE, HD),
            vmem(ROWS, 4 * HD),
            vmem(32, ROWS, dtype=F32),
            vmem(32, ROWS, dtype=F32),
            vmem(3, FR, 4 * HD),
            vmem(4, FR, HD),
            vmem(3, FR, HD),
            vmem(4, FR, HD, dtype=F32),
            vmem(4, FR, HD),
            vmem(3, FR, HD),
            vmem(4, FR, HD),
            vmem(4, 4, FR, HD),
            vmem(ROWS, 4 * HD),
            vmem(32, ROWS, dtype=F32),
            vmem(32, ROWS, dtype=F32),
            vmem(HD, ROWS, dtype=F32),
            vmem(4, HD, dtype=F32),
            pltpu.SMEM((1,), jnp.int32),
            pltpu.SemaphoreType.REGULAR,
            pltpu.SemaphoreType.DMA((SENT,)),
            pltpu.SemaphoreType.DMA((CAME,)),
            pltpu.SemaphoreType.DMA((16,)),
        ],
        compiler_params=pltpu.CompilerParams(
            collective_id=0, has_side_effects=True, vmem_limit_bytes=56 << 20
        ),
        cost_estimate=pl.CostEstimate(
            flops=4 * 2 * 256 * D * 512, bytes_accessed=8 << 20, transcendentals=0
        ),
    )(
        layer_input,
        cotangent,
        key_weight,
        key_gain.reshape(4, HD),
        fragment,
        outer_params.T,
        outer_momentum.T,
        plan,
    )
    new_weight, new_fragment, new_outer, new_moment = pl.pallas_call(
        hand_over,
        out_shape=[jax.ShapeDtypeStruct(a.shape, a.dtype) for a in results],
        in_specs=[any_spec] * 4,
        out_specs=[any_spec] * 4,
        scratch_shapes=[pltpu.VMEM(a.shape, a.dtype) for a in results]
        + [pltpu.SemaphoreType.DMA((4,))] * 2,
    )(*results)
    return new_weight, new_fragment, new_outer.T, new_moment.T


def hand_over(*refs):
    n = (len(refs) - 2) // 3
    came, gone = refs[-2:]
    loads = [pltpu.make_async_copy(refs[i], refs[2 * n + i], came.at[i]) for i in range(n)]
    stores = [pltpu.make_async_copy(refs[2 * n + i], refs[n + i], gone.at[i]) for i in range(n)]
    for copy in loads:
        copy.start()
    for load, store in zip(loads, stores):
        load.wait()
        store.start()
    for copy in stores:
        copy.wait()


def solution(mesh):
    placed = (
        P("rep", None, "fsdp", None),
        P("rep", None, "fsdp", None),
        P("rep", "fsdp", None),
        P(),
        P("rep", "fsdp", None),
        P("fsdp", "rep"),
        P("fsdp", "rep"),
        P(),
    )
    return jax.shard_map(
        shards,
        mesh=mesh,
        in_specs=placed,
        out_specs=(
            P("rep", "fsdp", None),
            P("rep", "fsdp", None),
            P("fsdp", "rep"),
            P("fsdp", "rep"),
        ),
        check_vma=False,
    )
```

```python
import functools
import math

import jax
import jax.numpy as jnp
from jax import lax
from jax.experimental import pallas as pl
from jax.experimental.pallas import tpu as pltpu
from jax.sharding import PartitionSpec as P

D = 5120
HD = 128
STEPS = 2
ROUNDS = 64
MOMENTUM_DECAY = 0.9
OUTER_RATE = 0.7
LOCAL_SHARE = 0.25

ORDER = (
    1, 0, 2, 51, 3, 4, 5, 50, 200, 7, 6, 9, 8, 12, 13, 10, 11, 53, 54, 55,
    52, 56, 57, 62, 14, 15, 16, 31, 201, 58, 60, 59, 61, 17, 18, 63, 64, 20, 21, 22,
    65, 66, 81, 19, 24, 23, 25, 67, 26, 27, 70, 68, 71, 72, 28, 73, 69, 101, 202, 29,
    100, 74, 75, 102, 76, 77, 103, 104, 105, 203, 106, 107, 78, 151, 79, 150, 112, 109, 111, 110,
    108, 152, 113, 114, 204, 153, 154, 155, 156, 157, 162, 115, 116, 131, 163, 159, 160, 158, 161, 117,
    118, 164, 121, 122, 165, 166, 181, 167, 168, 120, 119, 205, 171, 172, 170, 127, 174, 124, 173, 123,
    125, 169, 126, 177, 175, 176, 206, 128, 129, 178, 130, 179, 180,
)

MESH = pl.DeviceIdType.MESH
F32, BF16 = jnp.float32, jnp.bfloat16
NY, NZ = 4, 2
TOK = 256
ROWS = 320
SHARE = 2 * ROWS
CUT = 384
TOP = 384
SENT, CAME = 15, 55
FR = 80


def add(*terms):
    total = terms[0].astype(F32)
    for term in terms[1:]:
        total = total + term.astype(F32)
    return total


def kernel(
    inner_rate,
    x_hbm,
    c_hbm,
    w_hbm,
    gain_hbm,
    f_hbm,
    op_hbm,
    om_hbm,
    plan_hbm,
    ow_hbm,
    of_hbm,
    oo_hbm,
    omn_hbm,
    xb,
    cb,
    wg,
    keys,
    slope_t,
    gp,
    gq,
    rp1,
    rp2,
    tpz,
    rp3,
    rq1,
    rq2,
    rq3,
    wout,
    fr,
    opb,
    omb,
    rf1,
    tf2,
    rf2,
    rf3,
    tf4,
    rf4,
    rf5,
    rf6,
    fout,
    oob,
    omnb,
    side,
    gain_ref,
    plan_ref,
    relay,
    send_sems,
    recv_sems,
    local_sems,
):
    rep, fs = lax.axis_index("rep"), lax.axis_index("fsdp")
    z, y, c = fs // 8, (fs // 2) % 4, fs % 2
    zh, x = rep // 4, rep % 4
    yp, ym, y2 = (y + 1) % 4, (y + 3) % 4, (y + 2) % 4
    zo, co = 1 - z, 1 - c

    def dev(dz=z, dy=y, dc=c):
        return (rep, dz * 8 + dy * 2 + dc)

    up, down, across, twin = dev(dy=yp), dev(dy=ym), dev(dz=zo), dev(dc=co)
    xs = [(x + d) % 4 for d in (1, 2, 3)]
    zs = [(zh + d) % 4 for d in (1, 2, 3)]
    xdev = [(zh * 4 + i, fs) for i in xs]
    zdev = [(i * 4 + x, fs) for i in zs]

    locals_started, came_at, sent_at = [], {}, {}

    def remote(src, dst, sent, came, to=twin):
        return pltpu.make_async_remote_copy(
            src_ref=src,
            dst_ref=dst,
            send_sem=send_sems.at[sent_at.setdefault(sent, len(sent_at))],
            recv_sem=recv_sems.at[came_at.setdefault(came, len(came_at))],
            device_id=to,
            device_id_type=MESH,
        )

    def send(src, dst, to, sent, came):
        remote(src, dst, sent, came, to).start()

    def landed(ref, came):
        remote(ref, ref, "x0", came).wait_recv()

    def left(ref, sent):
        remote(ref, ref, sent, "x0").wait_send()

    def local(src, dst):
        copy = pltpu.make_async_copy(src, dst, local_sems.at[len(locals_started)])
        copy.start()
        locals_started.append(copy)
        return copy

    def columns(head):
        return pl.ds(pl.multiple_of(head * HD, HD), HD)

    half = lambda core: pl.ds(pl.multiple_of(core * 2 * HD, 2 * HD), 2 * HD)
    own_rows = pl.ds(pl.multiple_of(c * ROWS, 64), ROWS)
    other_rows = pl.ds(pl.multiple_of(co * ROWS, 64), ROWS)

    barrier = pltpu.get_barrier_semaphore()
    plane = [(rep, z * 8 + yp * 2), (rep, z * 8 + ym * 2), (rep, zo * 8 + y * 2)]
    depth = [(i * 4 + x, z * 8 + y * 2 + 1) for i in zs]
    depth += [(zh * 4 + i, z * 8 + y * 2 + 1) for i in xs]
    for to in plane + depth:
        pl.semaphore_signal(barrier, inc=1, device_id=to, device_id_type=MESH)

    @pl.when(c == 1)
    def _():
        pl.semaphore_signal(barrier, inc=1, device_id=twin, device_id_type=MESH)

    w_local = [local(w_hbm.at[0, :, columns(2 * c + h)], wg.at[0, h, z, y, own_rows, :]) for h in range(2)]
    x_local = [local(x_hbm.at[0, 0], xb.at[0, pl.ds(0, TOK), :]), None]
    c_local = [local(c_hbm.at[0, s, :, half(c)], cb.at[s, pl.ds(0, TOK), :]) for s in range(STEPS)]
    x_local[1] = local(x_hbm.at[0, 1], xb.at[1, pl.ds(0, TOK), :])
    f_local = local(f_hbm.at[0], fr)
    op_local = local(op_hbm, opb)
    om_local = local(om_hbm, omb)
    gain_local = local(gain_hbm, gain_ref)
    plan_local = local(plan_hbm, plan_ref)

    @pl.when(c == 0)
    def _():
        pl.semaphore_wait(barrier, 2 * len(plane) + 1)
        pl.semaphore_signal(relay, inc=1, device_id=twin, device_id_type=MESH)

    @pl.when(c == 1)
    def _():
        pl.semaphore_wait(relay, 1)

    def meet_depth():
        @pl.when(c == 1)
        def _():
            pl.semaphore_wait(barrier, 2 * len(depth))
            pl.semaphore_signal(relay, inc=1, device_id=twin, device_id_type=MESH)

        @pl.when(c == 0)
        def _():
            pl.semaphore_wait(relay, 1)

    for h in range(2):
        dst = wg.at[0, h, z, y, own_rows, :]
        send(w_hbm.at[0, :, columns(2 * co + h)], dst, twin, "ws", "ws")
    send(x_hbm.at[0, 0], xb.at[0, pl.ds(TOK, TOK), :], twin, "x0", "x0")
    for s in range(STEPS):
        send(c_hbm.at[0, s, :, half(co)], cb.at[s, pl.ds(TOK, TOK), :], twin, "c", "c")
    send(x_hbm.at[0, 1], xb.at[1, pl.ds(TOK, TOK), :], twin, "x1", "x1")

    todo = {}
    lo, hi = pl.ds(0, HD // 2), pl.ds(HD // 2, HD // 2)
    groups = dict(puu="k3", pdd="k3", qdz="k3", quz="k3", quuz="k4", qddz="k4", pzuu="k4", pzdd="k4",
                  Pu1="rp", Pu2="rp", Pd1="rp", Pd2="rp", z0="uq", Qu1="uq", Qu2="uq", Qd1="uq", Qd2="uq")

    def inner(s, h):
        k, mine = "AB"[h], "AB"[h] + str(s)
        w, sl = wg.at[s, h], slope_t.at[h]
        mp, mq = gp.at[s, h], gq.at[s, h]
        p1, p2, p3, pz = rp1.at[s, h], rp2.at[s, h], rp3.at[s, h], tpz.at[s, h]
        q1, q2, q3 = rq1.at[s, h], rq2.at[s, h], rq3.at[s, h]
        acc = keys.at[h]
        first, rest = (0, TOP), (TOP, SHARE - TOP)
        hp, hq = TOP // 2, (SHARE - TOP) // 2

        def push(name, bz, by, at, size, to):
            ref = w.at[bz, by, pl.ds(at, size), :]
            send(ref, ref, to, mine, k + groups.get(name, name))

        def put(name, src, dst, to):
            send(src, dst, to, mine, k + groups.get(name, name))

        def take(name, ref):
            landed(ref, k + name)

        def rows(at, size):
            return w.at[z, y, pl.ds(at, size), :]

        def g_p():
            push("pz", z, y, *first, across)
            push("pu", z, y, *first, up)
            push("pd", z, y, *first, down)

        def g_q():
            push("qu", z, y, *rest, up)
            push("qd", z, y, *rest, down)

        def g_z():
            push("qz", z, y, *rest, across)

        def a_qu():
            take("qu", rows(*rest))
            push("quu", z, ym, TOP, hq, up)
            push("quz", z, ym, *rest, across)

        def a_qd():
            take("qd", rows(*rest))
            push("qdd", z, yp, TOP + hq, hq, down)
            push("qdz", z, yp, *rest, across)

        def a_pz():
            take("pz", rows(*first))
            push("pzu", zo, y, *first, up)
            push("pzd", zo, y, *first, down)

        def a_pu():
            take("pu", rows(*first))
            push("puu", z, ym, 0, hp, up)

        def a_pd():
            take("pd", rows(*first))
            push("pdd", z, yp, hp, hp, down)

        def a_quu():
            take("quu", rows(TOP, hq))
            push("quuz", z, y2, TOP, hq, across)

        def a_qdd():
            take("qdd", rows(TOP, hq))
            push("qddz", z, y2, TOP + hq, hq, across)

        def a_pzu():
            take("pzu", rows(*first))
            push("pzuu", zo, ym, 0, hp, up)

        def a_pzd():
            take("pzd", rows(*first))
            push("pzdd", zo, yp, hp, hp, down)

        def project(*blocks):
            at = [pl.ds(pl.multiple_of((bz * NY + by) * SHARE, HD), SHARE) for bz, by in blocks]
            lhs = jnp.concatenate([xb[s, :, cols] for cols in at], axis=1)
            rhs = jnp.concatenate([w[bz, by] for bz, by in blocks], axis=0)
            return jnp.dot(lhs, rhs, preferred_element_type=F32)

        def k1():
            if h == 0:
                x_local[s].wait()
                landed(xb.at[s, pl.ds(TOK, TOK), :], "x" + str(s))
            acc[...] = project((z, y), (z, yp))

        def k2():
            take("qz", rows(*rest))
            acc[...] += project((z, ym), (zo, y))

        def k3():
            take("k3", cb.at[0, pl.ds(0, (2 * SHARE - TOP) // 2), :])
            acc[...] += project((z, y2), (zo, yp), (zo, ym))

        def k4():
            take("k4", w.at[z, y])
            if h == 0 and s == 0:
                c_local[0].wait()
                c_local[1].wait()
                landed(cb.at[0], "c")
                gain_local.wait()
            kv = (acc[...] + project((zo, y2))) * D**-0.5
            inverse = lax.rsqrt(jnp.mean(kv * kv, axis=-1, keepdims=True) + 1e-06)
            u = kv * inverse
            gain = gain_ref[pl.ds(2 * c + h, 1), :]
            pulled = cb[s, :, h * HD : (h + 1) * HD].astype(F32) * gain
            slope = (pulled - u * jnp.mean(pulled * u, axis=-1, keepdims=True)) * inverse
            sl[...] = slope.T.astype(BF16)

        def one(bz, by):
            at = pl.multiple_of((bz * NY + by) * SHARE, HD)
            part = jnp.dot(sl[...], xb[s, :, pl.ds(at, SHARE)], preferred_element_type=F32)
            mp[bz, by] = part[:, :CUT].astype(BF16)
            mq[bz, by] = part[:, CUT:].astype(BF16)

        def grad(by):
            def step(bz, carry):
                one(bz, by)
                return carry

            lax.fori_loop(0, NZ, step, 0)

        def g2():
            one(zo, y2)
            put("z2", mq.at[zo, y2], q1.at[y2], across)

        def g2b():
            one(z, y2)
            put("Pu", mp.at[:, y2, lo], p1.at[0], up)
            put("Pd", mp.at[:, y2, hi], p1.at[1], down)

        def gu():
            grad(yp)
            put("zp", mq.at[zo, yp], q1.at[yp], across)
            put("Pu1", mp.at[:, yp, hi], p2.at[0, :, hi], up)

        def gd():
            grad(ym)
            put("zm", mq.at[zo, ym], q1.at[ym], across)
            put("Pd1", mp.at[:, ym, lo], p2.at[1, :, lo], down)

        def g0():
            grad(y)
            put("z0", mq.at[zo, y], q1.at[y], across)

        def r_z2():
            take("z2", q1.at[y2])
            q1[y2] = add(q1[y2], mq[z, y2]).astype(BF16)
            put("Qu", q1.at[y2, lo], q2.at[0], up)
            put("Qd", q1.at[y2, hi], q2.at[1], down)

        def r_pu():
            take("Pu", p1.at[0])
            p1[0] = add(p1[0], mp[:, yp, lo]).astype(BF16)
            put("Pu2", p1.at[0], p2.at[0, :, lo], up)

        def r_pd():
            take("Pd", p1.at[1])
            p1[1] = add(p1[1], mp[:, ym, hi]).astype(BF16)
            put("Pd2", p1.at[1], p2.at[1, :, hi], down)

        def r_zp():
            take("zp", q1.at[yp])
            q1[yp] = add(q1[yp], mq[z, yp]).astype(BF16)
            put("Qu1", q1.at[yp, hi], q3.at[0, hi], up)

        def r_zm():
            take("zm", q1.at[ym])
            q1[ym] = add(q1[ym], mq[z, ym]).astype(BF16)
            put("Qd1", q1.at[ym, lo], q3.at[1, lo], down)

        def r_qu():
            take("Qu", q2.at[0])
            q1[yp, lo] = add(q1[yp, lo], q2[0]).astype(BF16)
            put("Qu2", q1.at[yp, lo], q3.at[0, lo], up)

        def r_qd():
            take("Qd", q2.at[1])
            q1[ym, hi] = add(q1[ym, hi], q2[1]).astype(BF16)
            put("Qd2", q1.at[ym, hi], q3.at[1, hi], down)

        def r_p():
            take("rp", p2)
            pz[...] = add(mp[zo, y], p2[0, zo], p2[1, zo]).astype(BF16)
            put("zl", pz, p3, across)

        old = w.at[z, y]
        new = wg.at[1, h, z, y] if s + 1 < STEPS else wout.at[h]
        scale = inner_rate * D**-0.5

        def uq():
            take("uq", q1.at[pl.ds(0, 3)])
            total = add(mq[z, y], q1[y], q3[0], q3[1])
            new[CUT:, :] = (old[CUT:, :].astype(F32) - scale * total.T).astype(BF16)

        def up_():
            take("zl", p3)
            total = add(mp[z, y], p2[0, z], p2[1, z], p3[...])
            new[:CUT, :] = (old[:CUT, :].astype(F32) - scale * total.T).astype(BF16)

        def write():
            src, cols = wout.at[h], columns(2 * c + h)
            local(src.at[own_rows, :], ow_hbm.at[0, :, cols])
            send(src.at[other_rows, :], ow_hbm.at[0, :, cols], twin, "w", "w")

        steps = dict(
            gp=g_p, gq=g_q, gz=g_z, a_qu=a_qu, a_qd=a_qd, a_pz=a_pz, a_pu=a_pu, a_pd=a_pd,
            a_quu=a_quu, a_qdd=a_qdd, a_pzu=a_pzu, a_pzd=a_pzd, k1=k1, k2=k2, k3=k3, k4=k4,
            g2=g2, gu=gu, gd=gd, g0=g0, r_z2=r_z2, r_pu=r_pu, r_pd=r_pd, r_zp=r_zp, r_zm=r_zm,
            r_qu=r_qu, r_qd=r_qd, r_p=r_p, uq=uq, up=up_, w=write, g2b=g2b,
        )
        for i, step in enumerate(steps.values()):
            todo[100 * s + 50 * h + i] = step

    for s in range(STEPS):
        for h in range(2):
            inner(s, h)

    def outer_0():
        meet_depth()
        for n, (i, to) in enumerate(zip(xs, xdev)):
            src = f_hbm.at[0, pl.ds(pl.multiple_of(i * FR, 16), FR), :]
            send(src, rf1.at[n], to, "a", "a")

    def outer_1():
        f_local.wait()
        landed(rf1, "a")
        mine = fr[pl.ds(pl.multiple_of(x * FR, 16), FR), :]
        total = add(mine, rf1[0], rf1[1], rf1[2]).astype(BF16)
        for i in range(4):
            tf2[i] = total[:, i * HD : (i + 1) * HD]
        for n, (i, to) in enumerate(zip(zs, zdev)):
            send(tf2.at[i], rf2.at[n], to, "b", "b")

    def outer_2():
        landed(rf2, "b")
        rf3[x] = add(tf2[zh], rf2[0], rf2[1], rf2[2])
        for to in xdev:
            send(rf3.at[x], rf3.at[x], to, "g", "g")

    def outer_3():
        op_local.wait()
        om_local.wait()
        plan_local.wait()
        landed(rf3.at[pl.ds(0, 3)], "g")
        plan = jnp.full((8, HD), plan_ref[0].astype(F32))
        factor = (OUTER_RATE * (0.55 + 0.45 * jnp.cos(math.pi * plan / ROUNDS)))[:1, :1]
        mine = pl.ds(pl.multiple_of(x * 32, 32), 32)
        side[...] = rf3[...].reshape(ROWS, HD).T
        pseudo = opb[...] - side[mine, :] * (1.0 / 16)
        moment = MOMENTUM_DECAY * omb[...] + pseudo
        new = opb[...] - factor * (pseudo + MOMENTUM_DECAY * moment)
        oob[...] = new
        omnb[...] = moment
        side[...] = jnp.zeros_like(side)
        side[mine, :] = new
        tf4[...] = side[...].T.astype(BF16).reshape(4, FR, HD)
        local(oob, oo_hbm)
        local(omnb, omn_hbm)
        for n, (i, to) in enumerate(zip(xs, xdev)):
            send(tf4.at[i], rf4.at[n], to, "d", "d")

    def outer_4():
        landed(rf4, "d")
        rf5[zh] = add(tf4[x], rf4[0], rf4[1], rf4[2]).astype(BF16)
        for to in zdev:
            send(rf5.at[zh], rf5.at[zh], to, "e", "e")

    def outer_5():
        landed(rf5.at[pl.ds(0, 3)], "e")
        for to in xdev:
            send(rf5, rf6.at[x], to, "f", "f")
        rf6[x] = rf5[...]

    def outer_6():
        landed(rf6.at[pl.ds(0, 3)], "f")
        for i in range(4):
            for j in range(4):
                rows, cols = slice(i * FR, (i + 1) * FR), slice(j * HD, (j + 1) * HD)
                blend = LOCAL_SHARE * fr[rows, cols].astype(F32)
                blend = blend + (1.0 - LOCAL_SHARE) * rf6[i, j].astype(F32)
                fout[rows, cols] = blend.astype(BF16)
        local(fout, of_hbm.at[0])

    for i, step in enumerate((outer_0, outer_1, outer_2, outer_3, outer_4, outer_5, outer_6)):
        todo[200 + i] = step
    for copy in w_local:
        copy.wait()
    landed(wg.at[0, 0, z, y], "ws")
    for number in ORDER:
        todo[number]()
    two_heads = ow_hbm.at[0, :, pl.ds(0, 2 * HD)]
    landed(two_heads, "w")
    for copy in locals_started[11:]:
        copy.wait()
    for sent in ("A0", "B0", "A1", "B1"):
        left(xb.at[0, pl.ds(0, 14 * SHARE * HD // D), :], sent)
    left(wg.at[0, 0, z, y], "ws")
    left(two_heads, "w")
    left(cb.at[0], "c")
    for s in range(STEPS):
        left(xb.at[s, pl.ds(TOK, TOK), :], "x" + str(s))
    for sent, ref in (("a", rf1), ("b", rf2), ("g", rf3.at[pl.ds(0, 3)]), ("d", rf4),
                      ("e", rf5.at[pl.ds(0, 3)]), ("f", rf6.at[pl.ds(0, 3)])):
        left(ref, sent)


def shards(
    layer_input, cotangent, key_weight, key_gain, fragment, outer_params, outer_momentum, plan
):
    tokens = layer_input.shape[2] * lax.axis_size("fsdp")
    inner_rate = 0.5 * math.sqrt(D / tokens)
    any_spec = pl.BlockSpec(memory_space=pl.ANY)
    vmem = lambda *shape, dtype=BF16: pltpu.VMEM(shape, dtype)
    hc, zr = HD // 2, SHARE - CUT
    results = pl.pallas_call(
        functools.partial(kernel, inner_rate),
        out_shape=(
            jax.ShapeDtypeStruct(key_weight.shape, BF16),
            jax.ShapeDtypeStruct(fragment.shape, BF16),
            jax.ShapeDtypeStruct(outer_params.shape[::-1], F32),
            jax.ShapeDtypeStruct(outer_momentum.shape[::-1], F32),
        ),
        in_specs=[any_spec] * 8,
        out_specs=[any_spec] * 4,
        scratch_shapes=[
            vmem(STEPS, 2 * TOK, D),
            vmem(STEPS, 2 * TOK, 2 * HD),
            vmem(STEPS, 2, NZ, NY, SHARE, HD),
            vmem(2, 2 * TOK, HD, dtype=F32),
            vmem(2, HD, 2 * TOK),
            vmem(STEPS, 2, NZ, NY, HD, CUT),
            vmem(STEPS, 2, NZ, NY, HD, zr),
            vmem(STEPS, 2, 2, NZ, hc, CUT),
            vmem(STEPS, 2, 2, NZ, HD, CUT),
            vmem(STEPS, 2, HD, CUT),
            vmem(STEPS, 2, HD, CUT),
            vmem(STEPS, 2, NY, HD, zr),
            vmem(STEPS, 2, 2, hc, zr),
            vmem(STEPS, 2, 2, HD, zr),
            vmem(2, SHARE, HD),
            vmem(ROWS, 4 * HD),
            vmem(32, ROWS, dtype=F32),
            vmem(32, ROWS, dtype=F32),
            vmem(3, FR, 4 * HD),
            vmem(4, FR, HD),
            vmem(3, FR, HD),
            vmem(4, FR, HD, dtype=F32),
            vmem(4, FR, HD),
            vmem(3, FR, HD),
            vmem(4, FR, HD),
            vmem(4, 4, FR, HD),
            vmem(ROWS, 4 * HD),
            vmem(32, ROWS, dtype=F32),
            vmem(32, ROWS, dtype=F32),
            vmem(HD, ROWS, dtype=F32),
            vmem(4, HD, dtype=F32),
            pltpu.SMEM((1,), jnp.int32),
            pltpu.SemaphoreType.REGULAR,
            pltpu.SemaphoreType.DMA((SENT,)),
            pltpu.SemaphoreType.DMA((CAME,)),
            pltpu.SemaphoreType.DMA((16,)),
        ],
        compiler_params=pltpu.CompilerParams(
            collective_id=0, has_side_effects=True, vmem_limit_bytes=56 << 20
        ),
        cost_estimate=pl.CostEstimate(
            flops=4 * 2 * 256 * D * 512, bytes_accessed=8 << 20, transcendentals=0
        ),
    )(
        layer_input,
        cotangent,
        key_weight,
        key_gain.reshape(4, HD),
        fragment,
        outer_params.T,
        outer_momentum.T,
        plan,
    )
    new_weight, new_fragment, new_outer, new_moment = pl.pallas_call(
        hand_over,
        out_shape=[jax.ShapeDtypeStruct(a.shape, a.dtype) for a in results],
        in_specs=[any_spec] * 4,
        out_specs=[any_spec] * 4,
        scratch_shapes=[pltpu.VMEM(a.shape, a.dtype) for a in results]
        + [pltpu.SemaphoreType.DMA((4,))] * 2,
    )(*results)
    return new_weight, new_fragment, new_outer.T, new_moment.T


def hand_over(*refs):
    n = (len(refs) - 2) // 3
    came, gone = refs[-2:]
    loads = [pltpu.make_async_copy(refs[i], refs[2 * n + i], came.at[i]) for i in range(n)]
    stores = [pltpu.make_async_copy(refs[2 * n + i], refs[n + i], gone.at[i]) for i in range(n)]
    for copy in loads:
        copy.start()
    for load, store in zip(loads, stores):
        load.wait()
        store.start()
    for copy in stores:
        copy.wait()


def solution(mesh):
    placed = (
        P("rep", None, "fsdp", None),
        P("rep", None, "fsdp", None),
        P("rep", "fsdp", None),
        P(),
        P("rep", "fsdp", None),
        P("fsdp", "rep"),
        P("fsdp", "rep"),
        P(),
    )
    return jax.shard_map(
        shards,
        mesh=mesh,
        in_specs=placed,
        out_specs=(
            P("rep", "fsdp", None),
            P("rep", "fsdp", None),
            P("fsdp", "rep"),
            P("fsdp", "rep"),
        ),
        check_vma=False,
    )
```

```python
import functools
import math

import jax
import jax.numpy as jnp
from jax import lax
from jax.experimental import pallas as pl
from jax.experimental.pallas import tpu as pltpu
from jax.sharding import PartitionSpec as P

D = 5120
HD = 128
STEPS = 2
ROUNDS = 64
MOMENTUM_DECAY = 0.9
OUTER_RATE = 0.7
LOCAL_SHARE = 0.25

ORDER = (
    1, 0, 2, 51, 3, 4, 5, 50, 200, 7, 6, 9, 8, 12, 13, 10, 11, 53, 54, 55,
    52, 56, 57, 62, 14, 15, 16, 31, 201, 58, 60, 59, 61, 17, 18, 63, 64, 20, 21, 22,
    65, 66, 81, 19, 24, 23, 25, 67, 26, 27, 70, 68, 71, 72, 28, 73, 69, 101, 202, 29,
    100, 74, 75, 102, 76, 77, 103, 104, 105, 203, 106, 107, 78, 151, 79, 150, 112, 109, 111, 110,
    108, 152, 113, 114, 204, 153, 154, 155, 156, 157, 162, 115, 116, 131, 163, 159, 160, 158, 161, 117,
    118, 164, 121, 122, 165, 166, 181, 167, 168, 120, 119, 205, 171, 172, 170, 127, 174, 124, 173, 123,
    125, 169, 126, 177, 175, 176, 206, 128, 129, 178, 130, 179, 180,
)

MESH = pl.DeviceIdType.MESH
F32, BF16 = jnp.float32, jnp.bfloat16
NY, NZ = 4, 2
TOK = 256
ROWS = 320
SHARE = 2 * ROWS
CUT = 384
TOP = 384
SENT, CAME = 15, 55
FR = 80


def add(*terms):
    total = terms[0].astype(F32)
    for term in terms[1:]:
        total = total + term.astype(F32)
    return total


def kernel(
    inner_rate,
    x_hbm,
    c_hbm,
    w_hbm,
    gain_hbm,
    f_hbm,
    op_hbm,
    om_hbm,
    plan_hbm,
    ow_hbm,
    of_hbm,
    oo_hbm,
    omn_hbm,
    xb,
    cb,
    wg,
    keys,
    slope_t,
    gp,
    gq,
    rp1,
    rp2,
    tpz,
    rp3,
    rq1,
    rq2,
    rq3,
    wout,
    fr,
    opb,
    omb,
    rf1,
    tf2,
    rf2,
    rf3,
    tf4,
    rf4,
    rf5,
    rf6,
    fout,
    oob,
    omnb,
    side,
    gain_ref,
    plan_ref,
    relay,
    send_sems,
    recv_sems,
    local_sems,
):
    rep, fs = lax.axis_index("rep"), lax.axis_index("fsdp")
    z, y, c = fs // 8, (fs // 2) % 4, fs % 2
    zh, x = rep // 4, rep % 4
    yp, ym, y2 = (y + 1) % 4, (y + 3) % 4, (y + 2) % 4
    zo, co = 1 - z, 1 - c

    def dev(dz=z, dy=y, dc=c):
        return (rep, dz * 8 + dy * 2 + dc)

    up, down, across, twin = dev(dy=yp), dev(dy=ym), dev(dz=zo), dev(dc=co)
    xs = [(x + d) % 4 for d in (1, 2, 3)]
    zs = [(zh + d) % 4 for d in (1, 2, 3)]
    xdev = [(zh * 4 + i, fs) for i in xs]
    zdev = [(i * 4 + x, fs) for i in zs]

    locals_started, came_at, sent_at = [], {}, {}

    def remote(src, dst, sent, came, to=twin):
        return pltpu.make_async_remote_copy(
            src_ref=src,
            dst_ref=dst,
            send_sem=send_sems.at[sent_at.setdefault(sent, len(sent_at))],
            recv_sem=recv_sems.at[came_at.setdefault(came, len(came_at))],
            device_id=to,
            device_id_type=MESH,
        )

    def send(src, dst, to, sent, came):
        remote(src, dst, sent, came, to).start()

    def landed(ref, came):
        remote(ref, ref, "x0", came).wait_recv()

    def left(ref, sent):
        remote(ref, ref, sent, "x0").wait_send()

    def local(src, dst):
        copy = pltpu.make_async_copy(src, dst, local_sems.at[len(locals_started)])
        copy.start()
        locals_started.append(copy)
        return copy

    def columns(head):
        return pl.ds(pl.multiple_of(head * HD, HD), HD)

    half = lambda core: pl.ds(pl.multiple_of(core * 2 * HD, 2 * HD), 2 * HD)
    own_rows = pl.ds(pl.multiple_of(c * ROWS, 64), ROWS)
    other_rows = pl.ds(pl.multiple_of(co * ROWS, 64), ROWS)

    barrier = pltpu.get_barrier_semaphore()
    plane = [(rep, z * 8 + yp * 2), (rep, z * 8 + ym * 2), (rep, zo * 8 + y * 2)]
    depth = [(i * 4 + x, z * 8 + y * 2 + 1) for i in zs]
    depth += [(zh * 4 + i, z * 8 + y * 2 + 1) for i in xs]
    for to in plane + depth:
        pl.semaphore_signal(barrier, inc=1, device_id=to, device_id_type=MESH)

    @pl.when(c == 1)
    def _():
        pl.semaphore_signal(barrier, inc=1, device_id=twin, device_id_type=MESH)

    w_local = [local(w_hbm.at[0, :, columns(2 * c + h)], wg.at[0, h, z, y, own_rows, :]) for h in range(2)]
    x_local = [local(x_hbm.at[0, 0], xb.at[0, pl.ds(0, TOK), :]), None]
    c_local = [local(c_hbm.at[0, s, :, half(c)], cb.at[s, pl.ds(0, TOK), :]) for s in range(STEPS)]
    x_local[1] = local(x_hbm.at[0, 1], xb.at[1, pl.ds(0, TOK), :])
    f_local = local(f_hbm.at[0], fr)
    op_local = local(op_hbm, opb)
    om_local = local(om_hbm, omb)
    gain_local = local(gain_hbm, gain_ref)
    plan_local = local(plan_hbm, plan_ref)

    @pl.when(c == 0)
    def _():
        pl.semaphore_wait(barrier, 2 * len(plane) + 1)
        pl.semaphore_signal(relay, inc=1, device_id=twin, device_id_type=MESH)

    @pl.when(c == 1)
    def _():
        pl.semaphore_wait(relay, 1)

    def meet_depth():
        @pl.when(c == 1)
        def _():
            pl.semaphore_wait(barrier, 2 * len(depth))
            pl.semaphore_signal(relay, inc=1, device_id=twin, device_id_type=MESH)

        @pl.when(c == 0)
        def _():
            pl.semaphore_wait(relay, 1)

    for h in range(2):
        dst = wg.at[0, h, z, y, own_rows, :]
        send(w_hbm.at[0, :, columns(2 * co + h)], dst, twin, "ws", "ws")
    send(x_hbm.at[0, 0], xb.at[0, pl.ds(TOK, TOK), :], twin, "x0", "x0")
    for s in range(STEPS):
        send(c_hbm.at[0, s, :, half(co)], cb.at[s, pl.ds(TOK, TOK), :], twin, "c", "c")
    send(x_hbm.at[0, 1], xb.at[1, pl.ds(TOK, TOK), :], twin, "x1", "x1")

    todo = {}
    lo, hi = pl.ds(0, HD // 2), pl.ds(HD // 2, HD // 2)
    groups = dict(puu="k3", pdd="k3", qdz="k3", quz="k3", quuz="k4", qddz="k4", pzuu="k4", pzdd="k4",
                  Pu1="rp", Pu2="rp", Pd1="rp", Pd2="rp", z0="uq", Qu1="uq", Qu2="uq", Qd1="uq", Qd2="uq")

    def inner(s, h):
        k, mine = "AB"[h], "AB"[h] + str(s)
        w, sl = wg.at[s, h], slope_t.at[h]
        mp, mq = gp.at[s, h], gq.at[s, h]
        p1, p2, p3, pz = rp1.at[s, h], rp2.at[s, h], rp3.at[s, h], tpz.at[s, h]
        q1, q2, q3 = rq1.at[s, h], rq2.at[s, h], rq3.at[s, h]
        acc = keys.at[h]
        first, rest = (0, TOP), (TOP, SHARE - TOP)
        hp, hq = TOP // 2, (SHARE - TOP) // 2

        def push(name, bz, by, at, size, to):
            ref = w.at[bz, by, pl.ds(at, size), :]
            send(ref, ref, to, mine, k + groups.get(name, name))

        def put(name, src, dst, to):
            send(src, dst, to, mine, k + groups.get(name, name))

        def take(name, ref):
            landed(ref, k + name)

        def rows(at, size):
            return w.at[z, y, pl.ds(at, size), :]

        def g_p():
            push("pz", z, y, *first, across)
            push("pu", z, y, *first, up)
            push("pd", z, y, *first, down)

        def g_q():
            push("qu", z, y, *rest, up)
            push("qd", z, y, *rest, down)

        def g_z():
            push("qz", z, y, *rest, across)

        def a_qu():
            take("qu", rows(*rest))
            push("quu", z, ym, TOP, hq, up)
            push("quz", z, ym, *rest, across)

        def a_qd():
            take("qd", rows(*rest))
            push("qdd", z, yp, TOP + hq, hq, down)
            push("qdz", z, yp, *rest, across)

        def a_pz():
            take("pz", rows(*first))
            push("pzu", zo, y, *first, up)
            push("pzd", zo, y, *first, down)

        def a_pu():
            take("pu", rows(*first))
            push("puu", z, ym, 0, hp, up)

        def a_pd():
            take("pd", rows(*first))
            push("pdd", z, yp, hp, hp, down)

        def a_quu():
            take("quu", rows(TOP, hq))
            push("quuz", z, y2, TOP, hq, across)

        def a_qdd():
            take("qdd", rows(TOP, hq))
            push("qddz", z, y2, TOP + hq, hq, across)

        def a_pzu():
            take("pzu", rows(*first))
            push("pzuu", zo, ym, 0, hp, up)

        def a_pzd():
            take("pzd", rows(*first))
            push("pzdd", zo, yp, hp, hp, down)

        def project(*blocks):
            at = [pl.ds(pl.multiple_of((bz * NY + by) * SHARE, HD), SHARE) for bz, by in blocks]
            lhs = jnp.concatenate([xb[s, :, cols] for cols in at], axis=1)
            rhs = jnp.concatenate([w[bz, by] for bz, by in blocks], axis=0)
            return jnp.dot(lhs, rhs, preferred_element_type=F32)

        def k1():
            if h == 0:
                x_local[s].wait()
                landed(xb.at[s, pl.ds(TOK, TOK), :], "x" + str(s))
            acc[...] = project((z, y), (z, yp))

        def k2():
            take("qz", rows(*rest))
            acc[...] += project((z, ym), (zo, y))

        def k3():
            take("k3", cb.at[0, pl.ds(0, (2 * SHARE - TOP) // 2), :])
            acc[...] += project((z, y2), (zo, yp), (zo, ym))

        def k4():
            take("k4", w.at[z, y])
            if h == 0 and s == 0:
                c_local[0].wait()
                c_local[1].wait()
                landed(cb.at[0], "c")
                gain_local.wait()
            kv = (acc[...] + project((zo, y2))) * D**-0.5
            inverse = lax.rsqrt(jnp.mean(kv * kv, axis=-1, keepdims=True) + 1e-06)
            u = kv * inverse
            gain = gain_ref[pl.ds(2 * c + h, 1), :]
            pulled = cb[s, :, h * HD : (h + 1) * HD].astype(F32) * gain
            slope = (pulled - u * jnp.mean(pulled * u, axis=-1, keepdims=True)) * inverse
            sl[...] = slope.T.astype(BF16)

        def one(bz, by):
            at = pl.multiple_of((bz * NY + by) * SHARE, HD)
            part = jnp.dot(sl[...], xb[s, :, pl.ds(at, SHARE)], preferred_element_type=F32)
            mp[bz, by] = part[:, :CUT].astype(BF16)
            mq[bz, by] = part[:, CUT:].astype(BF16)

        def grad(by):
            def step(bz, carry):
                one(bz, by)
                return carry

            lax.fori_loop(0, NZ, step, 0)

        def g2():
            one(zo, y2)
            put("z2", mq.at[zo, y2], q1.at[y2], across)

        def g2b():
            one(z, y2)
            put("Pu", mp.at[:, y2, lo], p1.at[0], up)
            put("Pd", mp.at[:, y2, hi], p1.at[1], down)

        def gu():
            grad(yp)
            put("zp", mq.at[zo, yp], q1.at[yp], across)
            put("Pu1", mp.at[:, yp, hi], p2.at[0, :, hi], up)

        def gd():
            grad(ym)
            put("zm", mq.at[zo, ym], q1.at[ym], across)
            put("Pd1", mp.at[:, ym, lo], p2.at[1, :, lo], down)

        def g0():
            grad(y)
            put("z0", mq.at[zo, y], q1.at[y], across)

        def r_z2():
            take("z2", q1.at[y2])
            q1[y2] = add(q1[y2], mq[z, y2]).astype(BF16)
            put("Qu", q1.at[y2, lo], q2.at[0], up)
            put("Qd", q1.at[y2, hi], q2.at[1], down)

        def r_pu():
            take("Pu", p1.at[0])
            p1[0] = add(p1[0], mp[:, yp, lo]).astype(BF16)
            put("Pu2", p1.at[0], p2.at[0, :, lo], up)

        def r_pd():
            take("Pd", p1.at[1])
            p1[1] = add(p1[1], mp[:, ym, hi]).astype(BF16)
            put("Pd2", p1.at[1], p2.at[1, :, hi], down)

        def r_zp():
            take("zp", q1.at[yp])
            q1[yp] = add(q1[yp], mq[z, yp]).astype(BF16)
            put("Qu1", q1.at[yp, hi], q3.at[0, hi], up)

        def r_zm():
            take("zm", q1.at[ym])
            q1[ym] = add(q1[ym], mq[z, ym]).astype(BF16)
            put("Qd1", q1.at[ym, lo], q3.at[1, lo], down)

        def r_qu():
            take("Qu", q2.at[0])
            q1[yp, lo] = add(q1[yp, lo], q2[0]).astype(BF16)
            put("Qu2", q1.at[yp, lo], q3.at[0, lo], up)

        def r_qd():
            take("Qd", q2.at[1])
            q1[ym, hi] = add(q1[ym, hi], q2[1]).astype(BF16)
            put("Qd2", q1.at[ym, hi], q3.at[1, hi], down)

        def r_p():
            take("rp", p2)
            pz[...] = add(mp[zo, y], p2[0, zo], p2[1, zo]).astype(BF16)
            put("zl", pz, p3, across)

        old = w.at[z, y]
        new = wg.at[1, h, z, y] if s + 1 < STEPS else wout.at[h]
        scale = inner_rate * D**-0.5

        def uq():
            take("uq", q1.at[pl.ds(0, 3)])
            total = add(mq[z, y], q1[y], q3[0], q3[1])
            new[CUT:, :] = (old[CUT:, :].astype(F32) - scale * total.T).astype(BF16)

        def up_():
            take("zl", p3)
            total = add(mp[z, y], p2[0, z], p2[1, z], p3[...])
            new[:CUT, :] = (old[:CUT, :].astype(F32) - scale * total.T).astype(BF16)

        def write():
            src, cols = wout.at[h], columns(2 * c + h)
            local(src.at[own_rows, :], ow_hbm.at[0, :, cols])
            send(src.at[other_rows, :], ow_hbm.at[0, :, cols], twin, "w", "w")

        steps = dict(
            gp=g_p, gq=g_q, gz=g_z, a_qu=a_qu, a_qd=a_qd, a_pz=a_pz, a_pu=a_pu, a_pd=a_pd,
            a_quu=a_quu, a_qdd=a_qdd, a_pzu=a_pzu, a_pzd=a_pzd, k1=k1, k2=k2, k3=k3, k4=k4,
            g2=g2, gu=gu, gd=gd, g0=g0, r_z2=r_z2, r_pu=r_pu, r_pd=r_pd, r_zp=r_zp, r_zm=r_zm,
            r_qu=r_qu, r_qd=r_qd, r_p=r_p, uq=uq, up=up_, w=write, g2b=g2b,
        )
        for i, step in enumerate(steps.values()):
            todo[100 * s + 50 * h + i] = step

    for s in range(STEPS):
        for h in range(2):
            inner(s, h)

    def outer_0():
        meet_depth()
        for n, (i, to) in enumerate(zip(xs, xdev)):
            src = f_hbm.at[0, pl.ds(pl.multiple_of(i * FR, 16), FR), :]
            send(src, rf1.at[n], to, "a", "a")

    def outer_1():
        f_local.wait()
        landed(rf1, "a")
        mine = fr[pl.ds(pl.multiple_of(x * FR, 16), FR), :]
        total = add(mine, rf1[0], rf1[1], rf1[2]).astype(BF16)
        for i in range(4):
            tf2[i] = total[:, i * HD : (i + 1) * HD]
        for n, (i, to) in enumerate(zip(zs, zdev)):
            send(tf2.at[i], rf2.at[n], to, "b", "b")

    def outer_2():
        landed(rf2, "b")
        rf3[x] = add(tf2[zh], rf2[0], rf2[1], rf2[2])
        for to in xdev:
            send(rf3.at[x], rf3.at[x], to, "g", "g")

    def outer_3():
        op_local.wait()
        om_local.wait()
        plan_local.wait()
        landed(rf3.at[pl.ds(0, 3)], "g")
        plan = jnp.full((8, HD), plan_ref[0].astype(F32))
        factor = (OUTER_RATE * (0.55 + 0.45 * jnp.cos(math.pi * plan / ROUNDS)))[:1, :1]
        mine = pl.ds(pl.multiple_of(x * 32, 32), 32)
        side[...] = rf3[...].reshape(ROWS, HD).T
        pseudo = opb[...] - side[mine, :] * (1.0 / 16)
        moment = MOMENTUM_DECAY * omb[...] + pseudo
        new = opb[...] - factor * (pseudo + MOMENTUM_DECAY * moment)
        oob[...] = new
        omnb[...] = moment
        side[...] = jnp.zeros_like(side)
        side[mine, :] = new
        tf4[...] = side[...].T.astype(BF16).reshape(4, FR, HD)
        local(oob, oo_hbm)
        local(omnb, omn_hbm)
        for n, (i, to) in enumerate(zip(xs, xdev)):
            send(tf4.at[i], rf4.at[n], to, "d", "d")

    def outer_4():
        landed(rf4, "d")
        rf5[zh] = add(tf4[x], rf4[0], rf4[1], rf4[2]).astype(BF16)
        for to in zdev:
            send(rf5.at[zh], rf5.at[zh], to, "e", "e")

    def outer_5():
        landed(rf5.at[pl.ds(0, 3)], "e")
        for to in xdev:
            send(rf5, rf6.at[x], to, "f", "f")
        rf6[x] = rf5[...]

    def outer_6():
        landed(rf6.at[pl.ds(0, 3)], "f")
        for i in range(4):
            for j in range(4):
                rows, cols = slice(i * FR, (i + 1) * FR), slice(j * HD, (j + 1) * HD)
                blend = LOCAL_SHARE * fr[rows, cols].astype(F32)
                blend = blend + (1.0 - LOCAL_SHARE) * rf6[i, j].astype(F32)
                fout[rows, cols] = blend.astype(BF16)
        local(fout, of_hbm.at[0])

    for i, step in enumerate((outer_0, outer_1, outer_2, outer_3, outer_4, outer_5, outer_6)):
        todo[200 + i] = step
    for copy in w_local:
        copy.wait()
    landed(wg.at[0, 0, z, y], "ws")
    for number in ORDER:
        todo[number]()
    two_heads = ow_hbm.at[0, :, pl.ds(0, 2 * HD)]
    landed(two_heads, "w")
    for copy in locals_started[11:]:
        copy.wait()
    for sent in ("A0", "B0", "A1", "B1"):
        left(xb.at[0, pl.ds(0, 14 * SHARE * HD // D), :], sent)
    left(wg.at[0, 0, z, y], "ws")
    left(two_heads, "w")
    left(cb.at[0], "c")
    for s in range(STEPS):
        left(xb.at[s, pl.ds(TOK, TOK), :], "x" + str(s))
    for sent, ref in (("a", rf1), ("b", rf2), ("g", rf3.at[pl.ds(0, 3)]), ("d", rf4),
                      ("e", rf5.at[pl.ds(0, 3)]), ("f", rf6.at[pl.ds(0, 3)])):
        left(ref, sent)


def shards(
    layer_input, cotangent, key_weight, key_gain, fragment, outer_params, outer_momentum, plan
):
    tokens = layer_input.shape[2] * lax.axis_size("fsdp")
    inner_rate = 0.5 * math.sqrt(D / tokens)
    any_spec = pl.BlockSpec(memory_space=pl.ANY)
    vmem = lambda *shape, dtype=BF16: pltpu.VMEM(shape, dtype)
    hc, zr = HD // 2, SHARE - CUT
    results = pl.pallas_call(
        functools.partial(kernel, inner_rate),
        out_shape=(
            jax.ShapeDtypeStruct(key_weight.shape, BF16),
            jax.ShapeDtypeStruct(fragment.shape, BF16),
            jax.ShapeDtypeStruct(outer_params.shape[::-1], F32),
            jax.ShapeDtypeStruct(outer_momentum.shape[::-1], F32),
        ),
        in_specs=[any_spec] * 8,
        out_specs=[any_spec] * 4,
        scratch_shapes=[
            vmem(STEPS, 2 * TOK, D),
            vmem(STEPS, 2 * TOK, 2 * HD),
            vmem(STEPS, 2, NZ, NY, SHARE, HD),
            vmem(2, 2 * TOK, HD, dtype=F32),
            vmem(2, HD, 2 * TOK),
            vmem(STEPS, 2, NZ, NY, HD, CUT),
            vmem(STEPS, 2, NZ, NY, HD, zr),
            vmem(STEPS, 2, 2, NZ, hc, CUT),
            vmem(STEPS, 2, 2, NZ, HD, CUT),
            vmem(STEPS, 2, HD, CUT),
            vmem(STEPS, 2, HD, CUT),
            vmem(STEPS, 2, NY, HD, zr),
            vmem(STEPS, 2, 2, hc, zr),
            vmem(STEPS, 2, 2, HD, zr),
            vmem(2, SHARE, HD),
            vmem(ROWS, 4 * HD),
            vmem(32, ROWS, dtype=F32),
            vmem(32, ROWS, dtype=F32),
            vmem(3, FR, 4 * HD),
            vmem(4, FR, HD),
            vmem(3, FR, HD),
            vmem(4, FR, HD, dtype=F32),
            vmem(4, FR, HD),
            vmem(3, FR, HD),
            vmem(4, FR, HD),
            vmem(4, 4, FR, HD),
            vmem(ROWS, 4 * HD),
            vmem(32, ROWS, dtype=F32),
            vmem(32, ROWS, dtype=F32),
            vmem(HD, ROWS, dtype=F32),
            vmem(4, HD, dtype=F32),
            pltpu.SMEM((1,), jnp.int32),
            pltpu.SemaphoreType.REGULAR,
            pltpu.SemaphoreType.DMA((SENT,)),
            pltpu.SemaphoreType.DMA((CAME,)),
            pltpu.SemaphoreType.DMA((16,)),
        ],
        compiler_params=pltpu.CompilerParams(
            collective_id=0, has_side_effects=True, vmem_limit_bytes=56 << 20
        ),
        cost_estimate=pl.CostEstimate(
            flops=4 * 2 * 256 * D * 512, bytes_accessed=8 << 20, transcendentals=0
        ),
    )(
        layer_input,
        cotangent,
        key_weight,
        key_gain.reshape(4, HD),
        fragment,
        outer_params.T,
        outer_momentum.T,
        plan,
    )
    new_weight, new_fragment, new_outer, new_moment = pl.pallas_call(
        hand_over,
        out_shape=[jax.ShapeDtypeStruct(a.shape, a.dtype) for a in results],
        in_specs=[any_spec] * 4,
        out_specs=[any_spec] * 4,
        scratch_shapes=[pltpu.VMEM(a.shape, a.dtype) for a in results]
        + [pltpu.SemaphoreType.DMA((6,))] * 2,
    )(*results)
    return new_weight, new_fragment, new_outer.T, new_moment.T


def hand_over(*refs):
    n = (len(refs) - 2) // 3
    came, gone = refs[-2:]
    parts = []
    for i in range(n):
        if len(refs[i].shape) == 3:
            size = refs[i].shape[1] // 2
            parts += [(i, (0, pl.ds(j * size, size))) for j in range(2)]
        else:
            parts.append((i, (slice(None),)))
    pick = lambda i, at: refs[i].at[at]
    loads = [
        pltpu.make_async_copy(pick(i, at), pick(2 * n + i, at), came.at[j])
        for j, (i, at) in enumerate(parts)
    ]
    stores = [
        pltpu.make_async_copy(pick(2 * n + i, at), pick(n + i, at), gone.at[j])
        for j, (i, at) in enumerate(parts)
    ]
    for copy in loads:
        copy.start()
    for load, store in zip(loads, stores):
        load.wait()
        store.start()
    for copy in stores:
        copy.wait()


def solution(mesh):
    placed = (
        P("rep", None, "fsdp", None),
        P("rep", None, "fsdp", None),
        P("rep", "fsdp", None),
        P(),
        P("rep", "fsdp", None),
        P("fsdp", "rep"),
        P("fsdp", "rep"),
        P(),
    )
    return jax.shard_map(
        shards,
        mesh=mesh,
        in_specs=placed,
        out_specs=(
            P("rep", "fsdp", None),
            P("rep", "fsdp", None),
            P("fsdp", "rep"),
            P("fsdp", "rep"),
        ),
        check_vma=False,
    )
```
